256 devices in a mesh: query: 16 (over x_lo, z), head: 16 (over y, x_hi, core).
Axes of the slice: x: 4 (x_hi: 2, x_lo: 2; x = x_hi * 2 + x_lo), y: 4, z: 8, core: 2. Of those that a mesh axis runs over, the one named last changes fastest.
Arguments:
- queries: bfloat16 [16384, 4096], P('query', 'head'), may hold values from -12 to 12
- mem_keys: bfloat16 [2048, 4096], P('head'), may hold values from -6 to 6
- mem_values: bfloat16 [2048, 4096], P('head'), may hold values from -6 to 6
- grad_out: bfloat16 [16384, 4096], P('query', 'head'), may hold values from -3 to 3
Outputs:
- attended: bfloat16 [16384, 4096], P('query', 'head')
- query_gradients: bfloat16 [16384, 4096], P('query', 'head')
- grad_keys: bfloat16 [2048, 4096], P(('query', 'head'))
- grad_values: bfloat16 [2048, 4096], P(('query', 'head'))
The draws below stay inside these ranges and needn't reach their ends.
All inputs are finite; a program needn't handle non-finite values.
Results may differ from the reference program's by a relative error of at most 0.025.
Values may be sent and summed in bfloat16 or wider, within the bound.
No kernel may reach another device: no remote copies, remote signals or barrier semaphores. Data moves between devices by JAX's collectives and lax.ppermute only.
A program may use at most 64 MiB of HBM per device.

```python
import jax
import jax.numpy as jnp
from jax import lax

HEADS = 16
HEAD_DIM = 256
WIDTH = 4096
ROWS = 16384
MEMORY = 2048


def draw_queries(key, part):
    key = jax.random.fold_in(key, 5)
    first_key = jax.random.fold_in(key, 0)
    values = jax.random.normal(first_key, (ROWS, WIDTH), jnp.float32) * 2.5
    return jnp.clip(values, -12.0, 12.0).astype(jnp.bfloat16)


def draw_mem_keys(key, part):
    key = jax.random.fold_in(key, 11)
    first_key = jax.random.fold_in(key, 0)
    values = jax.random.normal(first_key, (MEMORY, WIDTH), jnp.float32)
    return jnp.clip(values, -6.0, 6.0).astype(jnp.bfloat16)


def steps_of(rng, extent, shards, low, largest):
    gain, own = 1.0, jax.random.fold_in(rng, 6)
    for axis_at, parts in shards:
        steps = jnp.exp(jax.random.uniform(jax.random.fold_in(own, axis_at), (parts,), jnp.float32, low / len(shards), largest / len(shards)))
        gain = gain * jnp.repeat(steps, extent[axis_at] // parts).reshape([-1 if axis == axis_at else 1 for axis in range(len(extent))])
    return gain


def scatter_about(key, extent, scale, most, shards=(), dtype=jnp.bfloat16):
    values = jax.random.normal(key, extent, jnp.float32) * scale
    if len(shards) > 0:
        values = steps_of(key, extent, shards, -0.22, 0.18) * values
    return jnp.clip(values, min=-most, max=most).astype(dtype)


def setup_inputs(seed: int = 0) -> dict:
    arg_keys = jax.random.split(jax.random.key(seed), 5)
    queries = draw_queries(jax.random.fold_in(arg_keys[4], 71), 0)
    mem_keys = draw_mem_keys(jax.random.fold_in(arg_keys[4], 71), 0)
    mem_values = scatter_about(arg_keys[2], (MEMORY, WIDTH), 1.0, 6.0, ((0, 16),))
    grad_out = scatter_about(arg_keys[3], (ROWS, WIDTH), 0.5, 3.0, ((0, 16), (1, 16)))
    return {"queries": queries, "mem_keys": mem_keys, "mem_values": mem_values, "grad_out": grad_out}


def one_head(pieces):
    query_h, key_h, value_h, cotan_h = pieces
    score_scale = HEAD_DIM ** -0.5
    scores = jnp.dot(query_h, key_h.T, preferred_element_type=jnp.float32) * score_scale
    row_top = jnp.max(scores, axis=-1, keepdims=True)
    weights = jnp.exp(scores - row_top)
    attention_probabilities = (weights / jnp.sum(weights, axis=-1, keepdims=True)).astype(jnp.bfloat16)
    attended = jnp.dot(attention_probabilities, value_h, preferred_element_type=jnp.float32).astype(jnp.bfloat16)
    dprobs = jnp.dot(cotan_h, value_h.T, preferred_element_type=jnp.float32)
    row_delta = jnp.sum(attention_probabilities.astype(jnp.float32) * dprobs, axis=-1, keepdims=True)
    score_gradients = (attention_probabilities.astype(jnp.float32) * (dprobs - row_delta) * score_scale).astype(jnp.bfloat16)
    grad_query = jnp.dot(score_gradients, key_h, preferred_element_type=jnp.float32).astype(jnp.bfloat16)
    grad_key = jnp.dot(score_gradients.T, query_h, preferred_element_type=jnp.float32).astype(jnp.bfloat16)
    grad_value = jnp.dot(attention_probabilities.T, cotan_h, preferred_element_type=jnp.float32).astype(jnp.bfloat16)
    return attended, grad_query, grad_key, grad_value


def split_heads(array):
    return array.reshape(array.shape[0], HEADS, HEAD_DIM).transpose(1, 0, 2)


def join_heads(array):
    return array.transpose(1, 0, 2).reshape(array.shape[1], HEADS * HEAD_DIM)


def reference(queries, mem_keys, mem_values, grad_out):
    stacked = (split_heads(queries), split_heads(mem_keys), split_heads(mem_values), split_heads(grad_out))
    attended, query_gradients, grad_keys, grad_values = lax.map(one_head, stacked)
    return join_heads(attended), join_heads(query_gradients), join_heads(grad_keys), join_heads(grad_values)
```

```python
import functools
import itertools

import jax
import jax.numpy as jnp
from jax import lax
from jax.experimental import pallas as pl
from jax.experimental.pallas import tpu as pltpu
from jax.sharding import PartitionSpec as P

HEAD_DIM = 256
AXES = ("query", "head")
X_LO, Z, Y, X_HI, CORE = 2, 8, 4, 2, 2
TILE = 256
LOG2E = 1.4426950408889634


def device(xl, z, y, xh, c):
    return (xl * Z + z) * (Y * X_HI * CORE) + (y * X_HI + xh) * CORE + c


def permute(array, to):
    pairs = [
        (device(*at), device(*to(*at)))
        for at in itertools.product(range(X_LO), range(Z), range(Y), range(X_HI), range(CORE))
    ]
    return lax.ppermute(array, AXES, pairs)


def exchange(array, groups):
    return lax.all_to_all(
        array, AXES, split_axis=0, concat_axis=0, axis_index_groups=groups, tiled=True
    )


def swap_core_and_x_lo(xl, z, y, xh, c):
    return (c, z, y, xh, xl)


def other_core(xl, z, y, xh, c):
    return (xl, z, y, xh, 1 - c)


def head_groups():
    return [
        [device(xl, z, y, xh, c) for y in range(Y) for xh in range(X_HI)]
        for xl in range(X_LO)
        for z in range(Z)
        for c in range(CORE)
    ]


def z_groups():
    return [
        [device(xl, z, y, xh, c) for z in range(Z)]
        for xl in range(X_LO)
        for y in range(Y)
        for xh in range(X_HI)
        for c in range(CORE)
    ]


def column_groups():
    return [
        [device(xl, z, y, xh, c) for y in range(Y) for xh in range(X_HI) for xl in range(X_LO)]
        for z in range(Z)
        for c in range(CORE)
    ]


def pack_kernel(xl_ref, keys, values, out):
    out[0, 0] = keys[...]
    out[0, 1] = values[...]


def pack(xl, keys, values):
    rows = keys.shape[0]
    column = pl.BlockSpec((rows, HEAD_DIM), lambda chip, xl_ref: (0, chip * 2 + xl_ref[0]))
    return pl.pallas_call(
        pack_kernel,
        out_shape=jax.ShapeDtypeStruct((Y * X_HI, 2, rows, HEAD_DIM), keys.dtype),
        grid_spec=pltpu.PrefetchScalarGridSpec(
            num_scalar_prefetch=1,
            grid=(Y * X_HI,),
            in_specs=[column, column],
            out_specs=pl.BlockSpec((1, 2, rows, HEAD_DIM), lambda chip, xl_ref: (chip, 0, 0, 0)),
        ),
        name="pack",
    )(xl, keys, values)


def nt(a, b):
    return lax.dot_general(a, b, (((1,), (1,)), ((), ())), preferred_element_type=jnp.float32)


def nn(a, b):
    return jnp.dot(a, b, preferred_element_type=jnp.float32)


def attention_kernel(
    core_ref, q_ref, do_ref, own_ref, other_ref,
    att_ref, dq_ref, keep_ref, send_ref,
    k_ref, v_ref, kt_ref, vt_ref, s_ref, e_ref, dk_ref, dv_ref,
):
    core = core_ref[0]
    step = pl.program_id(0)
    memory = k_ref.shape[0]
    block = own_ref.shape[2]
    chunk = 256

    @pl.when(step == 0)
    def _():
        for chip in range(Y * X_HI):
            for source, at in ((own_ref, core), (other_ref, 1 - core)):
                rows = pl.ds(pl.multiple_of((chip * 2 + at) * block, block), block)
                k_ref[rows, :] = source[chip, 0]
                v_ref[rows, :] = source[chip, 1]
        for i in range(memory // chunk):
            rows = pl.ds(i * chunk, chunk)
            kt_ref[:, rows] = k_ref[rows, :].T
            vt_ref[:, rows] = v_ref[rows, :].T
        dk_ref[...] = jnp.zeros_like(dk_ref)
        dv_ref[...] = jnp.zeros_like(dv_ref)

    q = q_ref[...]
    do = do_ref[...]
    top = None
    for i in range(memory // chunk):
        rows = pl.ds(i * chunk, chunk)
        s = nt(k_ref[rows, :], q)
        s_ref[rows, :] = s
        here = jnp.max(s, axis=0, keepdims=True)
        top = here if top is None else jnp.maximum(top, here)
    factor = LOG2E * HEAD_DIM ** (-0.5)
    top = top * factor
    total = None
    att = None
    for i in range(memory // chunk):
        rows = pl.ds(i * chunk, chunk)
        e = jnp.exp2(s_ref[rows, :] * factor - top)
        here = jnp.sum(e, axis=0, keepdims=True)
        total = here if total is None else total + here
        eb = e.astype(jnp.bfloat16)
        e_ref[rows, :] = eb
        part = nn(vt_ref[:, rows], eb)
        att = part if att is None else att + part
    inverse = 1.0 / total
    att = att * inverse
    att_ref[...] = att.T.astype(jnp.bfloat16)
    dot = (do.astype(jnp.float32).T * inverse).astype(jnp.bfloat16)
    delta = jnp.sum(att * dot.astype(jnp.float32), axis=0, keepdims=True)
    dos = dot.T
    dq = None
    for i in range(memory // chunk):
        rows = pl.ds(i * chunk, chunk)
        dp = nn(v_ref[rows, :], dot)
        eb = e_ref[rows, :]
        ds = (eb.astype(jnp.float32) * (dp - delta)).astype(jnp.bfloat16)
        dv_ref[rows, :] += nn(eb, dos)
        dk_ref[rows, :] += nn(ds, q)
        part = nn(kt_ref[:, rows], ds)
        dq = part if dq is None else dq + part
    scale = HEAD_DIM ** (-0.5)
    dq_ref[...] = (dq * scale).T.astype(jnp.bfloat16)

    @pl.when(step == pl.num_programs(0) - 1)
    def _():
        for kind, (source, factor) in enumerate(((dk_ref, scale), (dv_ref, 1.0))):
            for xl in range(X_LO):
                for z in range(Z):
                    rows = pl.ds((xl * Z + z) * 128, 128)
                    full = source[rows, :].reshape(8, 2, 8, HEAD_DIM)
                    low = full[:, 0].reshape(64, HEAD_DIM) * factor
                    high = full[:, 1].reshape(64, HEAD_DIM) * factor
                    first = core == 0
                    at = pl.ds(xl * 64, 64)
                    keep_ref[z, kind, at, :] = jnp.where(first, low, high).astype(jnp.bfloat16)
                    send_ref[z, kind, at, :] = jnp.where(first, high, low).astype(jnp.bfloat16)


def attention(core, q, do, own, other):
    rows = q.shape[0]
    memory = 2 * own.shape[0] * own.shape[2]
    whole = lambda shape: pl.BlockSpec(shape, lambda i: (0,) * len(shape), memory_space=pltpu.VMEM)
    tile = pl.BlockSpec((TILE, HEAD_DIM), lambda i: (i, 0))
    parts = (Z, 2, memory // (2 * Z), HEAD_DIM)
    bf16, f32 = jnp.bfloat16, jnp.float32
    return pl.pallas_call(
        attention_kernel,
        grid=(rows // TILE,),
        out_shape=(
            jax.ShapeDtypeStruct((rows, HEAD_DIM), bf16),
            jax.ShapeDtypeStruct((rows, HEAD_DIM), bf16),
            jax.ShapeDtypeStruct(parts, bf16),
            jax.ShapeDtypeStruct(parts, bf16),
        ),
        in_specs=[
            pl.BlockSpec(memory_space=pltpu.SMEM),
            tile,
            tile,
            whole(own.shape),
            whole(other.shape),
        ],
        out_specs=(tile, tile, whole(parts), whole(parts)),
        scratch_shapes=[
            pltpu.VMEM((memory, HEAD_DIM), bf16),
            pltpu.VMEM((memory, HEAD_DIM), bf16),
            pltpu.VMEM((HEAD_DIM, memory), bf16),
            pltpu.VMEM((HEAD_DIM, memory), bf16),
            pltpu.VMEM((memory, TILE), f32),
            pltpu.VMEM((memory, TILE), bf16),
            pltpu.VMEM((memory, HEAD_DIM), f32),
            pltpu.VMEM((memory, HEAD_DIM), f32),
        ],
        compiler_params=pltpu.CompilerParams(
            dimension_semantics=("arbitrary",), vmem_limit_bytes=40 * 1024 * 1024
        ),
        cost_estimate=pl.CostEstimate(
            flops=12 * rows * memory * HEAD_DIM,
            bytes_accessed=8 * 1024 * 1024,
            transcendentals=rows * memory,
        ),
        name="attention",
    )(core, q, do, own, other)


def per_device(queries, mem_keys, mem_values, grad_out):
    xl = lax.axis_index("query") // Z
    core = lax.axis_index("head") % CORE
    as_ref = lambda value: jnp.reshape(value, (1,)).astype(jnp.int32)
    q = permute(queries, swap_core_and_x_lo)
    do = permute(grad_out, swap_core_and_x_lo)
    own = exchange(pack(as_ref(xl), mem_keys, mem_values), head_groups())
    other = permute(own, other_core)
    att, dq, keep, send = attention(as_ref(core), q, do, own, other)
    attended = permute(att, swap_core_and_x_lo)
    query_gradients = permute(dq, swap_core_and_x_lo)
    came = permute(send, other_core)
    chip_sum = (keep.astype(jnp.float32) + came.astype(jnp.float32)).astype(jnp.bfloat16)
    parts = exchange(chip_sum, z_groups())
    sums = jnp.sum(parts.astype(jnp.float32), axis=0).astype(jnp.bfloat16)
    sums = sums.reshape(2, X_LO, Y * X_HI, 8, HEAD_DIM).transpose(2, 1, 0, 3, 4)
    sums = sums.reshape(Y * X_HI * X_LO, 16, HEAD_DIM)
    final = exchange(sums, column_groups()).reshape(16, 2, 8, HEAD_DIM).transpose(1, 2, 0, 3)
    final = final.reshape(2, 8, 16 * HEAD_DIM)
    return attended, query_gradients, final[0], final[1]


def solution(mesh):
    in_specs = (P("query", "head"), P("head", None), P("head", None), P("query", "head"))
    out_specs = (
        P("query", "head"),
        P("query", "head"),
        P(("query", "head"), None),
        P(("query", "head"), None),
    )
    return jax.shard_map(
        per_device, mesh=mesh, in_specs=in_specs, out_specs=out_specs, check_vma=False
    )
```

```python
import functools
import itertools

import jax
import jax.numpy as jnp
from jax import lax
from jax.experimental import pallas as pl
from jax.experimental.pallas import tpu as pltpu
from jax.sharding import PartitionSpec as P

HEAD_DIM = 256
AXES = ("query", "head")
X_LO, Z, Y, X_HI, CORE = 2, 8, 4, 2, 2
CHUNK = 256
LOG2E = 1.4426950408889634


def device(xl, z, y, xh, c):
    return (xl * Z + z) * (Y * X_HI * CORE) + (y * X_HI + xh) * CORE + c


def permute(array, to):
    pairs = [
        (device(*at), device(*to(*at)))
        for at in itertools.product(range(X_LO), range(Z), range(Y), range(X_HI), range(CORE))
    ]
    return lax.ppermute(array, AXES, pairs)


def exchange(array, groups):
    return lax.all_to_all(
        array, AXES, split_axis=0, concat_axis=0, axis_index_groups=groups, tiled=True
    )


def trade(array):
    pairs = []
    for z, y, xh in itertools.product(range(Z), range(Y), range(X_HI)):
        one, two = device(0, z, y, xh, 1), device(1, z, y, xh, 0)
        pairs += [(one, two), (two, one)]
    return lax.ppermute(array, AXES, pairs)


def other_core(xl, z, y, xh, c):
    return (xl, z, y, xh, 1 - c)


def head_groups():
    return [
        [device(xl, z, y, xh, c) for y in range(Y) for xh in range(X_HI)]
        for xl in range(X_LO)
        for z in range(Z)
        for c in range(CORE)
    ]


def column_groups():
    return [
        [device(xl, z, y, xh, c) for y in range(Y) for xh in range(X_HI) for xl in range(X_LO)]
        for z in range(Z)
        for c in range(CORE)
    ]


SMEM = pl.BlockSpec(memory_space=pltpu.SMEM)
VMEM = pl.BlockSpec(memory_space=pltpu.VMEM)
ANY = pl.BlockSpec(memory_space=pl.ANY)
PARAMS = pltpu.CompilerParams(vmem_limit_bytes=32 * 1024 * 1024)
LARGE = pltpu.CompilerParams(vmem_limit_bytes=56 * 1024 * 1024)


def pack_kernel(xl_ref, keys, values, queries, cotangents, memory_out, rows_out, sems, row_sems):
    copies = []
    for chip in range(Y * X_HI):
        start = pl.multiple_of((chip * 2 + xl_ref[0]) * HEAD_DIM, HEAD_DIM)
        for kind, source in enumerate((keys, values)):
            copies.append(
                pltpu.make_async_copy(
                    source.at[:, pl.ds(start, HEAD_DIM)],
                    memory_out.at[chip, kind],
                    sems.at[chip, kind],
                )
            )
    for kind, source in enumerate((queries, cotangents)):
        copies.append(pltpu.make_async_copy(source, rows_out.at[kind], row_sems.at[kind]))
    for copy in copies:
        copy.start()
    for copy in copies:
        copy.wait()


def pack(xl, keys, values, queries, cotangents):
    rows = keys.shape[0]
    return pl.pallas_call(
        pack_kernel,
        out_shape=(
            jax.ShapeDtypeStruct((Y * X_HI, 2, rows, HEAD_DIM), keys.dtype),
            jax.ShapeDtypeStruct((2,) + queries.shape, queries.dtype),
        ),
        in_specs=[SMEM] + [ANY] * 4,
        out_specs=(VMEM, VMEM),
        scratch_shapes=[
            pltpu.SemaphoreType.DMA((Y * X_HI, 2)),
            pltpu.SemaphoreType.DMA((2,)),
        ],
        compiler_params=LARGE,
        name="pack",
    )(xl, keys, values, queries, cotangents)


def unpack_kernel(stay_ref, mine, came, attended, gradients, held, sems):
    def start(source):
        for kind in range(2):
            pltpu.make_async_copy(source.at[kind], held.at[kind], sems.at[0, kind]).start()

    pl.when(stay_ref[0] == 1)(lambda: start(mine))
    pl.when(stay_ref[0] == 0)(lambda: start(came))
    for kind, out in enumerate((attended, gradients)):
        pltpu.make_async_copy(came.at[kind], held.at[kind], sems.at[0, kind]).wait()
        pltpu.make_async_copy(held.at[kind], out, sems.at[1, kind]).start()
    for kind, out in enumerate((attended, gradients)):
        pltpu.make_async_copy(held.at[kind], out, sems.at[1, kind]).wait()


def unpack(stay, mine, came):
    out = jax.ShapeDtypeStruct(mine.shape[1:], mine.dtype)
    return pl.pallas_call(
        unpack_kernel,
        out_shape=(out, out),
        in_specs=[SMEM, ANY, ANY],
        out_specs=(ANY, ANY),
        scratch_shapes=[pltpu.VMEM(mine.shape, mine.dtype), pltpu.SemaphoreType.DMA((2, 2))],
        compiler_params=LARGE,
        name="unpack",
    )(stay, mine, came)


def core_sum_kernel(z_ref, keep, came, up, down, across, ahead, behind, own):
    def chunk(distance):
        at = lax.rem(z_ref[0] + distance, Z)
        return keep[at].astype(jnp.float32) + came[at].astype(jnp.float32)

    bf16 = jnp.bfloat16
    up[0] = chunk(3).astype(bf16)
    up[1] = chunk(1).astype(bf16)
    down[0] = chunk(5).astype(bf16)
    down[1] = chunk(7).astype(bf16)
    across[...] = chunk(4).astype(bf16)
    ahead[...] = chunk(2)
    behind[...] = chunk(6)
    own[...] = chunk(0)


def core_sum(z, keep, came):
    shape = keep.shape[1:]
    bf16, f32 = jnp.bfloat16, jnp.float32
    return pl.pallas_call(
        core_sum_kernel,
        out_shape=(
            jax.ShapeDtypeStruct((2,) + shape, bf16),
            jax.ShapeDtypeStruct((2,) + shape, bf16),
            jax.ShapeDtypeStruct(shape, bf16),
            jax.ShapeDtypeStruct(shape, f32),
            jax.ShapeDtypeStruct(shape, f32),
            jax.ShapeDtypeStruct(shape, f32),
        ),
        in_specs=[SMEM, VMEM, VMEM],
        out_specs=(VMEM,) * 6,
        compiler_params=PARAMS,
        name="core_sum",
    )(z, keep, came)


def middle_sum_kernel(core_ref, ahead, behind, from_below, from_above, across, up, down):
    far = across[...].astype(jnp.float32)
    first = core_ref[0] == 0
    zero = jnp.zeros_like(far)
    below = from_below[0].astype(jnp.float32) + jnp.where(first, far, zero)
    above = from_above[0].astype(jnp.float32) + jnp.where(first, zero, far)
    up[...] = (ahead[...] + below).astype(jnp.bfloat16)
    down[...] = (behind[...] + above).astype(jnp.bfloat16)


def middle_sum(core, ahead, behind, from_below, from_above, across):
    out = jax.ShapeDtypeStruct(ahead.shape, jnp.bfloat16)
    return pl.pallas_call(
        middle_sum_kernel,
        out_shape=(out, out),
        in_specs=[SMEM] + [VMEM] * 5,
        out_specs=(VMEM, VMEM),
        compiler_params=PARAMS,
        name="middle_sum",
    )(core, ahead, behind, from_below, from_above, across)


def last_sum_kernel(own, from_below, from_above, low, high, out):
    f32 = jnp.float32
    total = own[...] + from_below[1].astype(f32) + from_above[1].astype(f32)
    total = total + low[...].astype(f32) + high[...].astype(f32)
    total = total.reshape(2, X_LO, Y * X_HI, 8, HEAD_DIM)
    for xl in range(X_LO):
        for chip in range(Y * X_HI):
            both = jnp.concatenate([total[0, xl, chip], total[1, xl, chip]], axis=0)
            out[chip * 2 + xl] = both.astype(jnp.bfloat16)


def last_sum(own, from_below, from_above, low, high):
    return pl.pallas_call(
        last_sum_kernel,
        out_shape=jax.ShapeDtypeStruct((Y * X_HI * X_LO, 16, HEAD_DIM), jnp.bfloat16),
        in_specs=[VMEM] * 5,
        out_specs=VMEM,
        compiler_params=PARAMS,
        name="last_sum",
    )(own, from_below, from_above, low, high)


def columns_kernel(parts, keys, values):
    for head in range(Y * X_HI * X_LO):
        both = parts[head].astype(jnp.float32)
        at = pl.ds(head * HEAD_DIM, HEAD_DIM)
        keys[:, at] = both[:8].astype(jnp.bfloat16)
        values[:, at] = both[8:].astype(jnp.bfloat16)


def columns(parts):
    out = jax.ShapeDtypeStruct((8, parts.shape[0] * HEAD_DIM), jnp.bfloat16)
    return pl.pallas_call(
        columns_kernel,
        out_shape=(out, out),
        in_specs=[VMEM],
        out_specs=(VMEM, VMEM),
        compiler_params=PARAMS,
        name="columns",
    )(parts)


def sum_over_z(z, core, keep, came):
    above = lambda hops: lambda xl, z, y, xh, c: (xl, (z + hops) % Z, y, xh, c)
    over = lambda xl, z, y, xh, c: (xl, (z + (2 if c == 0 else 6)) % Z, y, xh, c)
    up, down, across, ahead, behind, own = core_sum(z, keep, came)
    from_below = permute(up, above(1))
    from_above = permute(down, above(7))
    far = permute(across, over)
    up, down = middle_sum(core, ahead, behind, from_below, from_above, far)
    low = permute(up, above(2))
    high = permute(down, above(6))
    return last_sum(own, from_below, from_above, low, high)


def nt(a, b):
    return lax.dot_general(a, b, (((1,), (1,)), ((), ())), preferred_element_type=jnp.float32)


def nn(a, b):
    return jnp.dot(a, b, preferred_element_type=jnp.float32)


def attention_kernel(
    core_ref, stay_ref, queries, cotangents, came, own, other,
    rows_out, keep_ref, send_ref,
    q_ref, do_ref, k_ref, v_ref, kt_ref, vt_ref, s_ref, e_ref, ds_ref, dos_ref, row_sems, sems,
):
    core = core_ref[0]
    memory = k_ref.shape[0]
    block = own.shape[2]

    def start_rows(q, do):
        pltpu.make_async_copy(q, q_ref, row_sems.at[0]).start()
        pltpu.make_async_copy(do, do_ref, row_sems.at[1]).start()

    pl.when(stay_ref[0] == 1)(lambda: start_rows(queries, cotangents))
    pl.when(stay_ref[0] == 0)(lambda: start_rows(came.at[0], came.at[1]))
    copies = [[], []]
    for kind, held in enumerate((k_ref, v_ref)):
        for chip in range(Y * X_HI):
            for side, (source, at) in enumerate(((own, core), (other, 1 - core))):
                rows = pl.ds(pl.multiple_of((chip * 2 + at) * block, block), block)
                copies[kind].append(
                    pltpu.make_async_copy(
                        source.at[chip, kind], held.at[rows], sems.at[kind, chip, side]
                    )
                )
                copies[kind][-1].start()
    pltpu.make_async_copy(queries, q_ref, row_sems.at[0]).wait()
    for copy in copies[0]:
        copy.wait()

    chunks = [pl.ds(i * CHUNK, CHUNK) for i in range(memory // CHUNK)]
    factor = LOG2E * HEAD_DIM ** (-0.5)
    scale = HEAD_DIM ** (-0.5)
    q = q_ref[...]
    top = None
    for rows in chunks:
        s = nt(k_ref[rows, :], q)
        s_ref[rows, :] = s
        here = jnp.max(s, axis=0, keepdims=True)
        top = here if top is None else jnp.maximum(top, here)
    top = top * factor
    for copy in copies[1]:
        copy.wait()
    for rows in chunks:
        kt_ref[:, rows] = k_ref[rows, :].T
        vt_ref[:, rows] = v_ref[rows, :].T
    total = None
    att = None
    for rows in chunks:
        e = jnp.exp2(s_ref[rows, :] * factor - top)
        here = jnp.sum(e, axis=0, keepdims=True)
        total = here if total is None else total + here
        eb = e.astype(jnp.bfloat16)
        e_ref[rows, :] = eb
        part = nn(vt_ref[:, rows], eb)
        att = part if att is None else att + part
    inverse = 1.0 / total
    att = att * inverse
    rows_out[0] = att.T.astype(jnp.bfloat16)
    pltpu.make_async_copy(cotangents, do_ref, row_sems.at[1]).wait()
    dot = (do_ref[...].astype(jnp.float32).T * inverse).astype(jnp.bfloat16)
    delta = jnp.sum(att * dot.astype(jnp.float32), axis=0, keepdims=True)
    dos_ref[...] = dot.T
    dq = None
    for rows in chunks:
        dp = nn(v_ref[rows, :], dot)
        ds = (e_ref[rows, :].astype(jnp.float32) * (dp - delta)).astype(jnp.bfloat16)
        ds_ref[rows, :] = ds
        part = nn(kt_ref[:, rows], ds)
        dq = part if dq is None else dq + part
    rows_out[1] = (dq * scale).T.astype(jnp.bfloat16)
    first = core == 0
    for i in range(memory // 256):
        rows = pl.ds(i * 256, 256)
        for kind, full in enumerate(
            (nn(ds_ref[rows, :], q_ref[...]) * scale, nn(e_ref[rows, :], dos_ref[...]))
        ):
            full = full.reshape(2, 8, 2, 8, HEAD_DIM)
            for half in range(2):
                xl, z = divmod(i * 2 + half, Z)
                low = full[half, :, 0].reshape(64, HEAD_DIM)
                high = full[half, :, 1].reshape(64, HEAD_DIM)
                at = pl.ds(xl * 64, 64)
                keep_ref[z, kind, at, :] = jnp.where(first, low, high).astype(jnp.bfloat16)
                send_ref[z, kind, at, :] = jnp.where(first, high, low).astype(jnp.bfloat16)


def attention(core, stay, queries, cotangents, came, own, other):
    rows = queries.shape[0]
    memory = 2 * own.shape[0] * own.shape[2]
    parts = (Z, 2, memory // (2 * Z), HEAD_DIM)
    bf16, f32 = jnp.bfloat16, jnp.float32
    return pl.pallas_call(
        attention_kernel,
        out_shape=(
            jax.ShapeDtypeStruct((2, rows, HEAD_DIM), bf16),
            jax.ShapeDtypeStruct(parts, bf16),
            jax.ShapeDtypeStruct(parts, bf16),
        ),
        in_specs=[SMEM, SMEM] + [ANY] * 5,
        out_specs=(VMEM, VMEM, VMEM),
        scratch_shapes=[
            pltpu.VMEM((rows, HEAD_DIM), bf16),
            pltpu.VMEM((rows, HEAD_DIM), bf16),
            pltpu.VMEM((memory, HEAD_DIM), bf16),
            pltpu.VMEM((memory, HEAD_DIM), bf16),
            pltpu.VMEM((HEAD_DIM, memory), bf16),
            pltpu.VMEM((HEAD_DIM, memory), bf16),
            pltpu.VMEM((memory, rows), f32),
            pltpu.VMEM((memory, rows), bf16),
            pltpu.VMEM((memory, rows), bf16),
            pltpu.VMEM((rows, HEAD_DIM), bf16),
            pltpu.SemaphoreType.DMA((2,)),
            pltpu.SemaphoreType.DMA((2, Y * X_HI, 2)),
        ],
        compiler_params=LARGE,
        cost_estimate=pl.CostEstimate(
            flops=12 * rows * memory * HEAD_DIM,
            bytes_accessed=8 * 1024 * 1024,
            transcendentals=rows * memory,
        ),
        name="attention",
    )(core, stay, queries, cotangents, came, own, other)


def per_device(queries, mem_keys, mem_values, grad_out):
    as_ref = lambda value: jnp.reshape(value, (1,)).astype(jnp.int32)
    xl = as_ref(lax.axis_index("query") // Z)
    z = as_ref(lax.axis_index("query") % Z)
    core = as_ref(lax.axis_index("head") % CORE)
    stay = (xl == core).astype(jnp.int32)
    memory, both = pack(xl, mem_keys, mem_values, queries, grad_out)
    both = trade(both)
    own = exchange(memory, head_groups())
    own, both = lax.optimization_barrier((own, both))
    other = permute(own, other_core)
    rows, keep, send = attention(core, stay, queries, grad_out, both, own, other)
    came = permute(send, other_core)
    traded = trade(rows)
    sums = sum_over_z(z, core, keep, came)
    attended, query_gradients = unpack(stay, rows, traded)
    grad_keys, grad_values = columns(exchange(sums, column_groups()))
    return attended, query_gradients, grad_keys, grad_values


def solution(mesh):
    in_specs = (P("query", "head"), P("head", None), P("head", None), P("query", "head"))
    out_specs = (
        P("query", "head"),
        P("query", "head"),
        P(("query", "head"), None),
        P(("query", "head"), None),
    )
    return jax.shard_map(
        per_device, mesh=mesh, in_specs=in_specs, out_specs=out_specs, check_vma=False
    )
```

```python
import functools
import itertools

import jax
import jax.numpy as jnp
from jax import lax
from jax.experimental import pallas as pl
from jax.experimental.pallas import tpu as pltpu
from jax.sharding import PartitionSpec as P

HEAD_DIM = 256
AXES = ("query", "head")
X_LO, Z, Y, X_HI, CORE = 2, 8, 4, 2, 2
SCALE = HEAD_DIM ** (-0.5)
CHUNK_CHIPS = 4
LOG2E = 1.4426950408889634


def position():
    query, head = lax.axis_index("query"), lax.axis_index("head")
    return lax.div(query, Z), lax.rem(query, Z), lax.rem(head, CORE)


def device(xl, z, y, xh, c):
    return (xl * Z + z) * (Y * X_HI * CORE) + (y * X_HI + xh) * CORE + c


def permute(array, to):
    pairs = [
        (device(*at), device(*to(*at)))
        for at in itertools.product(range(X_LO), range(Z), range(Y), range(X_HI), range(CORE))
    ]
    return lax.ppermute(array, AXES, pairs)


def exchange(array, groups):
    return lax.all_to_all(
        array, AXES, split_axis=0, concat_axis=0, axis_index_groups=groups, tiled=True
    )


def trade(array):
    pairs = []
    for z, y, xh in itertools.product(range(Z), range(Y), range(X_HI)):
        one, two = device(0, z, y, xh, 1), device(1, z, y, xh, 0)
        pairs += [(one, two), (two, one)]
    return lax.ppermute(array, AXES, pairs)


def other_core(xl, z, y, xh, c):
    return (xl, z, y, xh, 1 - c)


def head_groups():
    return [
        [device(xl, z, y, xh, c) for y in range(Y) for xh in range(X_HI)]
        for xl in range(X_LO)
        for z in range(Z)
        for c in range(CORE)
    ]


def column_groups():
    return [
        [device(xl, z, y, xh, c) for y in range(Y) for xh in range(X_HI) for xl in range(X_LO)]
        for z in range(Z)
        for c in range(CORE)
    ]


VMEM = pl.BlockSpec(memory_space=pltpu.VMEM)
ANY = pl.BlockSpec(memory_space=pl.ANY)


def params(mib):
    return pltpu.CompilerParams(vmem_limit_bytes=mib * 1024 * 1024)


def pack_kernel(keys, values, out, held, sems):
    xl, _, _ = position()
    copies = [
        pltpu.make_async_copy(source, held.at[kind], sems.at[kind])
        for kind, source in enumerate((keys, values))
    ]
    for copy in copies:
        copy.start()
    for kind, copy in enumerate(copies):
        copy.wait()
        for chip in range(Y * X_HI):
            start = pl.multiple_of((chip * 2 + xl) * HEAD_DIM, HEAD_DIM)
            out[chip, kind] = held[kind, :, pl.ds(start, HEAD_DIM)]


def pack(keys, values):
    shape = (Y * X_HI, 2, keys.shape[0], HEAD_DIM)
    return pl.pallas_call(
        pack_kernel,
        out_shape=jax.ShapeDtypeStruct(shape, keys.dtype),
        in_specs=[ANY, ANY],
        out_specs=VMEM,
        scratch_shapes=[
            pltpu.VMEM((2,) + keys.shape, keys.dtype),
            pltpu.SemaphoreType.DMA((2,)),
        ],
        compiler_params=params(56),
        name="pack",
    )(keys, values)


def select_kernel(queries, cotangents, q_came, do_came, q, do):
    xl, _, core = position()
    stay = xl == core
    q[...] = jnp.where(stay, queries[...], q_came[...])
    do[...] = jnp.where(stay, cotangents[...], do_came[...])


def select(queries, cotangents, q_came, do_came):
    out = jax.ShapeDtypeStruct(queries.shape, queries.dtype)
    return pl.pallas_call(
        select_kernel,
        out_shape=(out, out),
        in_specs=[VMEM] * 4,
        out_specs=(VMEM, VMEM),
        compiler_params=params(8),
        cost_estimate=pl.CostEstimate(flops=0, bytes_accessed=3 * 1024 * 1024, transcendentals=0),
        name="select",
    )(queries, cotangents, q_came, do_came)


def unpack_kernel(mine, came, attended, gradients):
    xl, _, core = position()
    stay = xl == core
    attended[...] = jnp.where(stay, mine[0], came[0])
    gradients[...] = jnp.where(stay, mine[1], came[1])


def unpack(mine, came):
    out = jax.ShapeDtypeStruct(mine.shape[1:], mine.dtype)
    return pl.pallas_call(
        unpack_kernel,
        out_shape=(out, out),
        in_specs=[VMEM, VMEM],
        out_specs=(VMEM, VMEM),
        compiler_params=params(12),
        name="unpack",
    )(mine, came)


def core_sum_kernel(keep, came, up, down, across, ahead, behind, own):
    _, z, _ = position()

    def chunk(distance):
        at = lax.rem(z + distance, Z)
        return keep[at].astype(jnp.float32) + came[at].astype(jnp.float32)

    bf16 = jnp.bfloat16
    up[0] = chunk(3).astype(bf16)
    up[1] = chunk(1).astype(bf16)
    down[0] = chunk(5).astype(bf16)
    down[1] = chunk(7).astype(bf16)
    across[...] = chunk(4).astype(bf16)
    ahead[...] = chunk(2)
    behind[...] = chunk(6)
    own[...] = chunk(0)


def core_sum(keep, came):
    shape = keep.shape[1:]
    bf16, f32 = jnp.bfloat16, jnp.float32
    return pl.pallas_call(
        core_sum_kernel,
        out_shape=(
            jax.ShapeDtypeStruct((2,) + shape, bf16),
            jax.ShapeDtypeStruct((2,) + shape, bf16),
            jax.ShapeDtypeStruct(shape, bf16),
            jax.ShapeDtypeStruct(shape, f32),
            jax.ShapeDtypeStruct(shape, f32),
            jax.ShapeDtypeStruct(shape, f32),
        ),
        in_specs=[VMEM, VMEM],
        out_specs=(VMEM,) * 6,
        compiler_params=params(12),
        name="core_sum",
    )(keep, came)


def middle_sum_kernel(ahead, behind, from_below, from_above, across, up, down):
    far = across[...].astype(jnp.float32)
    first = position()[2] == 0
    zero = jnp.zeros_like(far)
    below = from_below[0].astype(jnp.float32) + jnp.where(first, far, zero)
    above = from_above[0].astype(jnp.float32) + jnp.where(first, zero, far)
    up[...] = (ahead[...] + below).astype(jnp.bfloat16)
    down[...] = (behind[...] + above).astype(jnp.bfloat16)


def middle_sum(ahead, behind, from_below, from_above, across):
    out = jax.ShapeDtypeStruct(ahead.shape, jnp.bfloat16)
    return pl.pallas_call(
        middle_sum_kernel,
        out_shape=(out, out),
        in_specs=[VMEM] * 5,
        out_specs=(VMEM, VMEM),
        compiler_params=params(12),
        name="middle_sum",
    )(ahead, behind, from_below, from_above, across)


def last_sum_kernel(own, from_below, from_above, low, high, out):
    f32 = jnp.float32
    total = own[...] + from_below[1].astype(f32) + from_above[1].astype(f32)
    total = total + low[...].astype(f32) + high[...].astype(f32)
    total = total.reshape(2, X_LO, Y * X_HI, 8, HEAD_DIM)
    for xl in range(X_LO):
        for chip in range(Y * X_HI):
            both = jnp.concatenate([total[0, xl, chip], total[1, xl, chip]], axis=0)
            out[chip * 2 + xl] = both.astype(jnp.bfloat16)


def last_sum(own, from_below, from_above, low, high):
    return pl.pallas_call(
        last_sum_kernel,
        out_shape=jax.ShapeDtypeStruct((Y * X_HI * X_LO, 16, HEAD_DIM), jnp.bfloat16),
        in_specs=[VMEM] * 5,
        out_specs=VMEM,
        compiler_params=params(12),
        name="last_sum",
    )(own, from_below, from_above, low, high)


def columns_kernel(parts, keys, values):
    for head in range(Y * X_HI * X_LO):
        both = parts[head].astype(jnp.float32)
        at = pl.ds(head * HEAD_DIM, HEAD_DIM)
        keys[:, at] = both[:8].astype(jnp.bfloat16)
        values[:, at] = both[8:].astype(jnp.bfloat16)


def columns(parts):
    out = jax.ShapeDtypeStruct((8, parts.shape[0] * HEAD_DIM), jnp.bfloat16)
    return pl.pallas_call(
        columns_kernel,
        out_shape=(out, out),
        in_specs=[VMEM],
        out_specs=(VMEM, VMEM),
        compiler_params=params(12),
        name="columns",
    )(parts)


def sum_over_z(keep, came):
    above = lambda hops: lambda xl, z, y, xh, c: (xl, (z + hops) % Z, y, xh, c)
    over = lambda xl, z, y, xh, c: (xl, (z + (2 if c == 0 else 6)) % Z, y, xh, c)
    up, down, across, ahead, behind, own = core_sum(keep, came)
    from_below = permute(up, above(1))
    from_above = permute(down, above(7))
    far = permute(across, over)
    up, down = middle_sum(ahead, behind, from_below, from_above, far)
    low = permute(up, above(2))
    high = permute(down, above(6))
    return last_sum(own, from_below, from_above, low, high)


def nt(a, b):
    return lax.dot_general(a, b, (((1,), (1,)), ((), ())), preferred_element_type=jnp.float32)


def nn(a, b):
    return jnp.dot(a, b, preferred_element_type=jnp.float32)


def attention_kernel(
    queries, cotangents, own, other, rows_out, keep_ref, send_ref, s_ref, e_ref, ds_ref
):
    _, _, core = position()
    q = queries[...]
    do = cotangents[...]
    block = own.shape[2]
    chunks = [
        (source, at, chip)
        for source, at in ((own, core), (other, 1 - core))
        for chip in range(0, Y * X_HI, CHUNK_CHIPS)
    ]
    size = CHUNK_CHIPS * block
    places = [pl.ds(i * size, size) for i in range(len(chunks))]

    def rows_of(chunk, kind):
        source, _, chip = chunk
        return source[chip : chip + CHUNK_CHIPS, kind].reshape(size, HEAD_DIM)

    factor = LOG2E * SCALE
    top = None
    for chunk, rows in zip(chunks, places):
        s = nt(rows_of(chunk, 0), q)
        s_ref[rows, :] = s
        here = jnp.max(s, axis=0, keepdims=True)
        top = here if top is None else jnp.maximum(top, here)
    top = top * factor
    total = None
    att = None
    for chunk, rows in zip(chunks, places):
        e = jnp.exp2(s_ref[rows, :] * factor - top)
        here = jnp.sum(e, axis=0, keepdims=True)
        total = here if total is None else total + here
        eb = e.astype(jnp.bfloat16)
        e_ref[rows, :] = eb
        part = nn(rows_of(chunk, 1).T, eb)
        att = part if att is None else att + part
    inverse = 1.0 / total
    att = att * inverse
    rows_out[0] = att.T.astype(jnp.bfloat16)
    dot = (do.astype(jnp.float32).T * inverse).astype(jnp.bfloat16)
    delta = jnp.sum(att * dot.astype(jnp.float32), axis=0, keepdims=True)
    dos = dot.T
    dq = None
    for chunk, rows in zip(chunks, places):
        dp = nn(rows_of(chunk, 1), dot)
        ds = (e_ref[rows, :].astype(jnp.float32) * (dp - delta)).astype(jnp.bfloat16)
        ds_ref[rows, :] = ds
        part = nn(rows_of(chunk, 0).T, ds)
        dq = part if dq is None else dq + part
    rows_out[1] = (dq * SCALE).T.astype(jnp.bfloat16)
    first = core == 0
    for (_, side, first_chip), rows in zip(chunks, places):
        for kind, full in enumerate((nn(ds_ref[rows, :], q) * SCALE, nn(e_ref[rows, :], dos))):
            full = full.reshape(CHUNK_CHIPS, block // 16, 2, 8, HEAD_DIM)
            for i in range(CHUNK_CHIPS):
                xl, low_z = divmod(first_chip + i, Y * X_HI // X_LO)
                z = low_z * 2 + side
                low = full[i, :, 0].reshape(block // 2, HEAD_DIM)
                high = full[i, :, 1].reshape(block // 2, HEAD_DIM)
                at = pl.ds(xl * (block // 2), block // 2)
                keep_ref[z, kind, at, :] = jnp.where(first, low, high).astype(jnp.bfloat16)
                send_ref[z, kind, at, :] = jnp.where(first, high, low).astype(jnp.bfloat16)


def attention(queries, cotangents, own, other):
    rows = queries.shape[0]
    memory = 2 * own.shape[0] * own.shape[2]
    parts = (Z, 2, memory // (2 * Z), HEAD_DIM)
    bf16, f32 = jnp.bfloat16, jnp.float32
    return pl.pallas_call(
        attention_kernel,
        out_shape=(
            jax.ShapeDtypeStruct((2, rows, HEAD_DIM), bf16),
            jax.ShapeDtypeStruct(parts, bf16),
            jax.ShapeDtypeStruct(parts, bf16),
        ),
        in_specs=[VMEM] * 4,
        out_specs=(VMEM, VMEM, VMEM),
        scratch_shapes=[
            pltpu.VMEM((memory, rows), f32),
            pltpu.VMEM((memory, rows), bf16),
            pltpu.VMEM((memory, rows), bf16),
        ],
        compiler_params=params(24),
        cost_estimate=pl.CostEstimate(
            flops=12 * rows * memory * HEAD_DIM,
            bytes_accessed=8 * 1024 * 1024,
            transcendentals=rows * memory,
        ),
        name="attention",
    )(queries, cotangents, own, other)


def per_device(queries, mem_keys, mem_values, grad_out):
    q, do = select(queries, grad_out, trade(queries), trade(grad_out))
    own = exchange(pack(mem_keys, mem_values), head_groups())
    own, q, do = lax.optimization_barrier((own, q, do))
    other = permute(own, other_core)
    rows, keep, send = attention(q, do, own, other)
    came = permute(send, other_core)
    traded = trade(rows)
    sums = sum_over_z(keep, came)
    attended, query_gradients = unpack(rows, traded)
    grad_keys, grad_values = columns(exchange(sums, column_groups()))
    return attended, query_gradients, grad_keys, grad_values


def solution(mesh):
    in_specs = (P("query", "head"), P("head", None), P("head", None), P("query", "head"))
    out_specs = (
        P("query", "head"),
        P("query", "head"),
        P(("query", "head"), None),
        P(("query", "head"), None),
    )
    return jax.shard_map(
        per_device, mesh=mesh, in_specs=in_specs, out_specs=out_specs, check_vma=False
    )
```

```python
import functools
import itertools

import jax
import jax.numpy as jnp
from jax import lax
from jax.experimental import pallas as pl
from jax.experimental.pallas import tpu as pltpu
from jax.sharding import PartitionSpec as P

HEAD_DIM = 256
AXES = ("query", "head")
X_LO, Z, Y, X_HI, CORE = 2, 8, 4, 2, 2
SCALE = HEAD_DIM ** (-0.5)
CHUNK_CHIPS = 4
LOG2E = 1.4426950408889634


def position():
    query, head = lax.axis_index("query"), lax.axis_index("head")
    return lax.div(query, Z), lax.rem(query, Z), lax.rem(head, CORE)


def device(xl, z, y, xh, c):
    return (xl * Z + z) * (Y * X_HI * CORE) + (y * X_HI + xh) * CORE + c


def permute(array, to):
    pairs = [
        (device(*at), device(*to(*at)))
        for at in itertools.product(range(X_LO), range(Z), range(Y), range(X_HI), range(CORE))
    ]
    return lax.ppermute(array, AXES, pairs)


def exchange(array, groups):
    return lax.all_to_all(
        array, AXES, split_axis=0, concat_axis=0, axis_index_groups=groups, tiled=True
    )


def trade(array):
    pairs = []
    for z, y, xh in itertools.product(range(Z), range(Y), range(X_HI)):
        one, two = device(0, z, y, xh, 1), device(1, z, y, xh, 0)
        pairs += [(one, two), (two, one)]
    return lax.ppermute(array, AXES, pairs)


def other_core(xl, z, y, xh, c):
    return (xl, z, y, xh, 1 - c)


def head_groups():
    return [
        [device(xl, z, y, xh, c) for y in range(Y) for xh in range(X_HI)]
        for xl in range(X_LO)
        for z in range(Z)
        for c in range(CORE)
    ]


def column_groups():
    return [
        [device(xl, z, y, xh, c) for y in range(Y) for xh in range(X_HI) for xl in range(X_LO)]
        for z in range(Z)
        for c in range(CORE)
    ]


VMEM = pl.BlockSpec(memory_space=pltpu.VMEM)
ANY = pl.BlockSpec(memory_space=pl.ANY)


def params(mib):
    return pltpu.CompilerParams(vmem_limit_bytes=mib * 1024 * 1024)


def pack_kernel(keys, values, out, held, sems):
    xl, _, _ = position()
    copies = [
        pltpu.make_async_copy(source, held.at[kind], sems.at[kind])
        for kind, source in enumerate((keys, values))
    ]
    for copy in copies:
        copy.start()
    for kind, copy in enumerate(copies):
        copy.wait()
        for chip in range(Y * X_HI):
            start = pl.multiple_of((chip * 2 + xl) * HEAD_DIM, HEAD_DIM)
            out[chip, kind] = held[kind, :, pl.ds(start, HEAD_DIM)]


def pack(keys, values):
    shape = (Y * X_HI, 2, keys.shape[0], HEAD_DIM)
    return pl.pallas_call(
        pack_kernel,
        out_shape=jax.ShapeDtypeStruct(shape, keys.dtype),
        in_specs=[ANY, ANY],
        out_specs=VMEM,
        scratch_shapes=[
            pltpu.VMEM((2,) + keys.shape, keys.dtype),
            pltpu.SemaphoreType.DMA((2,)),
        ],
        compiler_params=params(56),
        name="pack",
    )(keys, values)


def select_kernel(queries, cotangents, q_came, do_came, q, do):
    xl, _, core = position()
    stay = xl == core
    q[...] = jnp.where(stay, queries[...], q_came[...])
    do[...] = jnp.where(stay, cotangents[...], do_came[...])


def select(queries, cotangents, q_came, do_came):
    out = jax.ShapeDtypeStruct(queries.shape, queries.dtype)
    return pl.pallas_call(
        select_kernel,
        out_shape=(out, out),
        in_specs=[VMEM] * 4,
        out_specs=(VMEM, VMEM),
        input_output_aliases={2: 0, 3: 1},
        compiler_params=params(8),
        cost_estimate=pl.CostEstimate(flops=0, bytes_accessed=3 * 1024 * 1024, transcendentals=0),
        name="select",
    )(queries, cotangents, q_came, do_came)


def unpack_kernel(mine, came, attended, gradients):
    xl, _, core = position()
    stay = xl == core
    attended[...] = jnp.where(stay, mine[0], came[0])
    gradients[...] = jnp.where(stay, mine[1], came[1])


def unpack(mine, came):
    out = jax.ShapeDtypeStruct(mine.shape[1:], mine.dtype)
    return pl.pallas_call(
        unpack_kernel,
        out_shape=(out, out),
        in_specs=[VMEM, VMEM],
        out_specs=(VMEM, VMEM),
        compiler_params=params(12),
        name="unpack",
    )(mine, came)


def core_sum_kernel(keep, came, up, down, across, ahead, behind, own):
    _, z, _ = position()

    def chunk(distance):
        at = lax.rem(z + distance, Z)
        return keep[at].astype(jnp.float32) + came[at].astype(jnp.float32)

    bf16 = jnp.bfloat16
    up[0] = chunk(3).astype(bf16)
    up[1] = chunk(1).astype(bf16)
    down[0] = chunk(5).astype(bf16)
    down[1] = chunk(7).astype(bf16)
    across[...] = chunk(4).astype(bf16)
    ahead[...] = chunk(2)
    behind[...] = chunk(6)
    own[...] = chunk(0)


def core_sum(keep, came):
    shape = keep.shape[1:]
    bf16, f32 = jnp.bfloat16, jnp.float32
    return pl.pallas_call(
        core_sum_kernel,
        out_shape=(
            jax.ShapeDtypeStruct((2,) + shape, bf16),
            jax.ShapeDtypeStruct((2,) + shape, bf16),
            jax.ShapeDtypeStruct(shape, bf16),
            jax.ShapeDtypeStruct(shape, f32),
            jax.ShapeDtypeStruct(shape, f32),
            jax.ShapeDtypeStruct(shape, f32),
        ),
        in_specs=[VMEM, VMEM],
        out_specs=(VMEM,) * 6,
        compiler_params=params(12),
        name="core_sum",
    )(keep, came)


def middle_sum_kernel(ahead, behind, from_below, from_above, across, up, down):
    far = across[...].astype(jnp.float32)
    first = position()[2] == 0
    zero = jnp.zeros_like(far)
    below = from_below[0].astype(jnp.float32) + jnp.where(first, far, zero)
    above = from_above[0].astype(jnp.float32) + jnp.where(first, zero, far)
    up[...] = (ahead[...] + below).astype(jnp.bfloat16)
    down[...] = (behind[...] + above).astype(jnp.bfloat16)


def middle_sum(ahead, behind, from_below, from_above, across):
    out = jax.ShapeDtypeStruct(ahead.shape, jnp.bfloat16)
    return pl.pallas_call(
        middle_sum_kernel,
        out_shape=(out, out),
        in_specs=[VMEM] * 5,
        out_specs=(VMEM, VMEM),
        compiler_params=params(12),
        name="middle_sum",
    )(ahead, behind, from_below, from_above, across)


def last_sum_kernel(own, from_below, from_above, low, high, out):
    f32 = jnp.float32
    total = own[...] + from_below[1].astype(f32) + from_above[1].astype(f32)
    total = total + low[...].astype(f32) + high[...].astype(f32)
    total = total.reshape(2, X_LO, Y * X_HI, 8, HEAD_DIM)
    for xl in range(X_LO):
        for chip in range(Y * X_HI):
            both = jnp.concatenate([total[0, xl, chip], total[1, xl, chip]], axis=0)
            out[chip * 2 + xl] = both.astype(jnp.bfloat16)


def last_sum(own, from_below, from_above, low, high):
    return pl.pallas_call(
        last_sum_kernel,
        out_shape=jax.ShapeDtypeStruct((Y * X_HI * X_LO, 16, HEAD_DIM), jnp.bfloat16),
        in_specs=[VMEM] * 5,
        out_specs=VMEM,
        compiler_params=params(12),
        name="last_sum",
    )(own, from_below, from_above, low, high)


def columns_kernel(parts, keys, values):
    for head in range(Y * X_HI * X_LO):
        both = parts[head].astype(jnp.float32)
        at = pl.ds(head * HEAD_DIM, HEAD_DIM)
        keys[:, at] = both[:8].astype(jnp.bfloat16)
        values[:, at] = both[8:].astype(jnp.bfloat16)


def columns(parts):
    out = jax.ShapeDtypeStruct((8, parts.shape[0] * HEAD_DIM), jnp.bfloat16)
    return pl.pallas_call(
        columns_kernel,
        out_shape=(out, out),
        in_specs=[VMEM],
        out_specs=(VMEM, VMEM),
        compiler_params=params(12),
        name="columns",
    )(parts)


def sum_over_z(keep, came):
    above = lambda hops: lambda xl, z, y, xh, c: (xl, (z + hops) % Z, y, xh, c)
    over = lambda xl, z, y, xh, c: (xl, (z + (2 if c == 0 else 6)) % Z, y, xh, c)
    up, down, across, ahead, behind, own = core_sum(keep, came)
    from_below = permute(up, above(1))
    from_above = permute(down, above(7))
    far = permute(across, over)
    up, down = middle_sum(ahead, behind, from_below, from_above, far)
    low = permute(up, above(2))
    high = permute(down, above(6))
    return last_sum(own, from_below, from_above, low, high)


def nt(a, b):
    return lax.dot_general(a, b, (((1,), (1,)), ((), ())), preferred_element_type=jnp.float32)


def nn(a, b):
    return jnp.dot(a, b, preferred_element_type=jnp.float32)


def attention_kernel(
    queries, cotangents, own, other, rows_out, keep_ref, send_ref, s_ref, e_ref, ds_ref
):
    _, _, core = position()
    q = queries[...]
    do = cotangents[...]
    block = own.shape[2]
    chunks = [
        (source, at, chip)
        for source, at in ((own, core), (other, 1 - core))
        for chip in range(0, Y * X_HI, CHUNK_CHIPS)
    ]
    size = CHUNK_CHIPS * block
    places = [pl.ds(i * size, size) for i in range(len(chunks))]

    def rows_of(chunk, kind):
        source, _, chip = chunk
        return source[chip : chip + CHUNK_CHIPS, kind].reshape(size, HEAD_DIM)

    factor = LOG2E * SCALE
    top = None
    for chunk, rows in zip(chunks, places):
        s = nt(rows_of(chunk, 0), q)
        s_ref[rows, :] = s
        here = jnp.max(s, axis=0, keepdims=True)
        top = here if top is None else jnp.maximum(top, here)
    top = top * factor
    total = None
    att = None
    for chunk, rows in zip(chunks, places):
        e = jnp.exp2(s_ref[rows, :] * factor - top)
        here = jnp.sum(e, axis=0, keepdims=True)
        total = here if total is None else total + here
        eb = e.astype(jnp.bfloat16)
        e_ref[rows, :] = eb
        part = nn(rows_of(chunk, 1).T, eb)
        att = part if att is None else att + part
    inverse = 1.0 / total
    att = att * inverse
    rows_out[0] = att.T.astype(jnp.bfloat16)
    dot = (do.astype(jnp.float32).T * inverse).astype(jnp.bfloat16)
    delta = jnp.sum(att * dot.astype(jnp.float32), axis=0, keepdims=True)
    dos = dot.T
    dq = None
    for chunk, rows in zip(chunks, places):
        dp = nn(rows_of(chunk, 1), dot)
        ds = (e_ref[rows, :].astype(jnp.float32) * (dp - delta)).astype(jnp.bfloat16)
        ds_ref[rows, :] = ds
        part = nn(rows_of(chunk, 0).T, ds)
        dq = part if dq is None else dq + part
    rows_out[1] = (dq * SCALE).T.astype(jnp.bfloat16)
    first = core == 0
    for (_, side, first_chip), rows in zip(chunks, places):
        for kind, full in enumerate((nn(ds_ref[rows, :], q) * SCALE, nn(e_ref[rows, :], dos))):
            full = full.reshape(CHUNK_CHIPS, block // 16, 2, 8, HEAD_DIM)
            for i in range(CHUNK_CHIPS):
                xl, low_z = divmod(first_chip + i, Y * X_HI // X_LO)
                z = low_z * 2 + side
                low = full[i, :, 0].reshape(block // 2, HEAD_DIM)
                high = full[i, :, 1].reshape(block // 2, HEAD_DIM)
                at = pl.ds(xl * (block // 2), block // 2)
                keep_ref[z, kind, at, :] = jnp.where(first, low, high).astype(jnp.bfloat16)
                send_ref[z, kind, at, :] = jnp.where(first, high, low).astype(jnp.bfloat16)


def attention(queries, cotangents, own, other):
    rows = queries.shape[0]
    memory = 2 * own.shape[0] * own.shape[2]
    parts = (Z, 2, memory // (2 * Z), HEAD_DIM)
    bf16, f32 = jnp.bfloat16, jnp.float32
    return pl.pallas_call(
        attention_kernel,
        out_shape=(
            jax.ShapeDtypeStruct((2, rows, HEAD_DIM), bf16),
            jax.ShapeDtypeStruct(parts, bf16),
            jax.ShapeDtypeStruct(parts, bf16),
        ),
        in_specs=[VMEM] * 4,
        out_specs=(VMEM, VMEM, VMEM),
        scratch_shapes=[
            pltpu.VMEM((memory, rows), f32),
            pltpu.VMEM((memory, rows), bf16),
            pltpu.VMEM((memory, rows), bf16),
        ],
        compiler_params=params(24),
        cost_estimate=pl.CostEstimate(
            flops=12 * rows * memory * HEAD_DIM,
            bytes_accessed=8 * 1024 * 1024,
            transcendentals=rows * memory,
        ),
        name="attention",
    )(queries, cotangents, own, other)


def per_device(queries, mem_keys, mem_values, grad_out):
    q_came = trade(queries)
    grad_out, q_came = lax.optimization_barrier((grad_out, q_came))
    q, do = select(queries, grad_out, q_came, trade(grad_out))
    own = exchange(pack(mem_keys, mem_values), head_groups())
    own, q, do = lax.optimization_barrier((own, q, do))
    other = permute(own, other_core)
    rows, keep, send = attention(q, do, own, other)
    came = permute(send, other_core)
    traded = trade(rows)
    sums = sum_over_z(keep, came)
    attended, query_gradients = unpack(rows, traded)
    grad_keys, grad_values = columns(exchange(sums, column_groups()))
    return attended, query_gradients, grad_keys, grad_values


def solution(mesh):
    in_specs = (P("query", "head"), P("head", None), P("head", None), P("query", "head"))
    out_specs = (
        P("query", "head"),
        P("query", "head"),
        P(("query", "head"), None),
        P(("query", "head"), None),
    )
    return jax.shard_map(
        per_device, mesh=mesh, in_specs=in_specs, out_specs=out_specs, check_vma=False
    )
```

```python
import functools
import itertools

import jax
import jax.numpy as jnp
from jax import lax
from jax.experimental import pallas as pl
from jax.experimental.pallas import tpu as pltpu
from jax.sharding import PartitionSpec as P

HEAD_DIM = 256
AXES = ("query", "head")
X_LO, Z, Y, X_HI, CORE = 2, 8, 4, 2, 2
SCALE = HEAD_DIM ** (-0.5)
CHUNK_CHIPS = 8
LOG2E = 1.4426950408889634


def position():
    query, head = lax.axis_index("query"), lax.axis_index("head")
    return lax.div(query, Z), lax.rem(query, Z), lax.rem(head, CORE)


def device(xl, z, y, xh, c):
    return (xl * Z + z) * (Y * X_HI * CORE) + (y * X_HI + xh) * CORE + c


def permute(array, to):
    pairs = [
        (device(*at), device(*to(*at)))
        for at in itertools.product(range(X_LO), range(Z), range(Y), range(X_HI), range(CORE))
    ]
    return lax.ppermute(array, AXES, pairs)


def exchange(array, groups):
    return lax.all_to_all(
        array, AXES, split_axis=0, concat_axis=0, axis_index_groups=groups, tiled=True
    )


def trade(array):
    pairs = []
    for z, y, xh in itertools.product(range(Z), range(Y), range(X_HI)):
        one, two = device(0, z, y, xh, 1), device(1, z, y, xh, 0)
        pairs += [(one, two), (two, one)]
    return lax.ppermute(array, AXES, pairs)


def other_core(xl, z, y, xh, c):
    return (xl, z, y, xh, 1 - c)


def head_groups():
    return [
        [device(xl, z, y, xh, c) for y in range(Y) for xh in range(X_HI)]
        for xl in range(X_LO)
        for z in range(Z)
        for c in range(CORE)
    ]


def column_groups():
    return [
        [device(xl, z, y, xh, c) for y in range(Y) for xh in range(X_HI) for xl in range(X_LO)]
        for z in range(Z)
        for c in range(CORE)
    ]


VMEM = pl.BlockSpec(memory_space=pltpu.VMEM)
ANY = pl.BlockSpec(memory_space=pl.ANY)


def params(mib):
    return pltpu.CompilerParams(vmem_limit_bytes=mib * 1024 * 1024)


def pack_kernel(keys, values, out, held, sems):
    xl, _, _ = position()
    copies = [
        pltpu.make_async_copy(source, held.at[kind], sems.at[kind])
        for kind, source in enumerate((keys, values))
    ]
    for copy in copies:
        copy.start()
    for kind, copy in enumerate(copies):
        copy.wait()
        for chip in range(Y * X_HI):
            start = pl.multiple_of((chip * 2 + xl) * HEAD_DIM, HEAD_DIM)
            out[chip, kind] = held[kind, :, pl.ds(start, HEAD_DIM)]


def pack(keys, values):
    shape = (Y * X_HI, 2, keys.shape[0], HEAD_DIM)
    return pl.pallas_call(
        pack_kernel,
        out_shape=jax.ShapeDtypeStruct(shape, keys.dtype),
        in_specs=[ANY, ANY],
        out_specs=VMEM,
        scratch_shapes=[
            pltpu.VMEM((2,) + keys.shape, keys.dtype),
            pltpu.SemaphoreType.DMA((2,)),
        ],
        compiler_params=params(56),
        name="pack",
    )(keys, values)


def select_kernel(queries, cotangents, q_came, do_came, q, do):
    xl, _, core = position()
    stay = xl == core
    q[...] = jnp.where(stay, queries[...], q_came[...])
    do[...] = jnp.where(stay, cotangents[...], do_came[...])


def select(queries, cotangents, q_came, do_came):
    out = jax.ShapeDtypeStruct(queries.shape, queries.dtype)
    return pl.pallas_call(
        select_kernel,
        out_shape=(out, out),
        in_specs=[VMEM] * 4,
        out_specs=(VMEM, VMEM),
        input_output_aliases={2: 0, 3: 1},
        compiler_params=params(8),
        cost_estimate=pl.CostEstimate(flops=0, bytes_accessed=3 * 1024 * 1024, transcendentals=0),
        name="select",
    )(queries, cotangents, q_came, do_came)


def unpack_kernel(mine, came, attended, gradients):
    xl, _, core = position()
    stay = xl == core
    attended[...] = jnp.where(stay, mine[0], came[0])
    gradients[...] = jnp.where(stay, mine[1], came[1])


def unpack(mine, came):
    out = jax.ShapeDtypeStruct(mine.shape[1:], mine.dtype)
    return pl.pallas_call(
        unpack_kernel,
        out_shape=(out, out),
        in_specs=[VMEM, VMEM],
        out_specs=(VMEM, VMEM),
        compiler_params=params(12),
        name="unpack",
    )(mine, came)


def core_sum_kernel(keep, came, up, down, across, ahead, behind, own):
    _, z, _ = position()

    def chunk(distance):
        at = lax.rem(z + distance, Z)
        return keep[at].astype(jnp.float32) + came[at].astype(jnp.float32)

    bf16 = jnp.bfloat16
    up[0] = chunk(3).astype(bf16)
    up[1] = chunk(1).astype(bf16)
    down[0] = chunk(5).astype(bf16)
    down[1] = chunk(7).astype(bf16)
    across[...] = chunk(4).astype(bf16)
    ahead[...] = chunk(2)
    behind[...] = chunk(6)
    own[...] = chunk(0)


def core_sum(keep, came):
    shape = keep.shape[1:]
    bf16, f32 = jnp.bfloat16, jnp.float32
    return pl.pallas_call(
        core_sum_kernel,
        out_shape=(
            jax.ShapeDtypeStruct((2,) + shape, bf16),
            jax.ShapeDtypeStruct((2,) + shape, bf16),
            jax.ShapeDtypeStruct(shape, bf16),
            jax.ShapeDtypeStruct(shape, f32),
            jax.ShapeDtypeStruct(shape, f32),
            jax.ShapeDtypeStruct(shape, f32),
        ),
        in_specs=[VMEM, VMEM],
        out_specs=(VMEM,) * 6,
        compiler_params=params(12),
        name="core_sum",
    )(keep, came)


def middle_sum_kernel(ahead, behind, from_below, from_above, across, up, down):
    far = across[...].astype(jnp.float32)
    first = position()[2] == 0
    zero = jnp.zeros_like(far)
    below = from_below[0].astype(jnp.float32) + jnp.where(first, far, zero)
    above = from_above[0].astype(jnp.float32) + jnp.where(first, zero, far)
    up[...] = (ahead[...] + below).astype(jnp.bfloat16)
    down[...] = (behind[...] + above).astype(jnp.bfloat16)


def middle_sum(ahead, behind, from_below, from_above, across):
    out = jax.ShapeDtypeStruct(ahead.shape, jnp.bfloat16)
    return pl.pallas_call(
        middle_sum_kernel,
        out_shape=(out, out),
        in_specs=[VMEM] * 5,
        out_specs=(VMEM, VMEM),
        compiler_params=params(12),
        name="middle_sum",
    )(ahead, behind, from_below, from_above, across)


def last_sum_kernel(own, from_below, from_above, low, high, out):
    f32 = jnp.float32
    total = own[...] + from_below[1].astype(f32) + from_above[1].astype(f32)
    total = total + low[...].astype(f32) + high[...].astype(f32)
    total = total.reshape(2, X_LO, Y * X_HI, 8, HEAD_DIM)
    for xl in range(X_LO):
        for chip in range(Y * X_HI):
            both = jnp.concatenate([total[0, xl, chip], total[1, xl, chip]], axis=0)
            out[chip * 2 + xl] = both.astype(jnp.bfloat16)


def last_sum(own, from_below, from_above, low, high):
    return pl.pallas_call(
        last_sum_kernel,
        out_shape=jax.ShapeDtypeStruct((Y * X_HI * X_LO, 16, HEAD_DIM), jnp.bfloat16),
        in_specs=[VMEM] * 5,
        out_specs=VMEM,
        compiler_params=params(12),
        name="last_sum",
    )(own, from_below, from_above, low, high)


def columns_kernel(parts, keys, values):
    for head in range(Y * X_HI * X_LO):
        both = parts[head].astype(jnp.float32)
        at = pl.ds(head * HEAD_DIM, HEAD_DIM)
        keys[:, at] = both[:8].astype(jnp.bfloat16)
        values[:, at] = both[8:].astype(jnp.bfloat16)


def columns(parts):
    out = jax.ShapeDtypeStruct((8, parts.shape[0] * HEAD_DIM), jnp.bfloat16)
    return pl.pallas_call(
        columns_kernel,
        out_shape=(out, out),
        in_specs=[VMEM],
        out_specs=(VMEM, VMEM),
        compiler_params=params(12),
        name="columns",
    )(parts)


def sum_over_z(keep, came):
    above = lambda hops: lambda xl, z, y, xh, c: (xl, (z + hops) % Z, y, xh, c)
    over = lambda xl, z, y, xh, c: (xl, (z + (2 if c == 0 else 6)) % Z, y, xh, c)
    up, down, across, ahead, behind, own = core_sum(keep, came)
    from_below = permute(up, above(1))
    from_above = permute(down, above(7))
    far = permute(across, over)
    up, down = middle_sum(ahead, behind, from_below, from_above, far)
    low = permute(up, above(2))
    high = permute(down, above(6))
    return last_sum(own, from_below, from_above, low, high)


def nt(a, b):
    return lax.dot_general(a, b, (((1,), (1,)), ((), ())), preferred_element_type=jnp.float32)


def nn(a, b):
    return jnp.dot(a, b, preferred_element_type=jnp.float32)


def half_chunks(source):
    size = CHUNK_CHIPS * source.shape[2]
    found = []
    for chip in range(0, Y * X_HI, CHUNK_CHIPS):
        load = lambda kind, chip=chip: source[chip : chip + CHUNK_CHIPS, kind].reshape(
            size, HEAD_DIM
        )
        found.append((pl.ds(len(found) * size, size), load, chip))
    return found


def scores_of(chunks, q, s_ref):
    top = None
    for rows, load, _ in chunks:
        s = nt(load(0), q)
        s_ref[rows, :] = s
        here = jnp.max(s, axis=0, keepdims=True)
        top = here if top is None else jnp.maximum(top, here)
    return top * (LOG2E * SCALE)


def weights_of(chunks, top, s_ref, e_ref):
    total, att = 0.0, 0.0
    for rows, load, _ in chunks:
        e = jnp.exp2(s_ref[rows, :] * (LOG2E * SCALE) - top)
        total = total + jnp.sum(e, axis=0, keepdims=True)
        eb = e.astype(jnp.bfloat16)
        e_ref[rows, :] = eb
        att = att + nn(load(1).T, eb)
    return total, att


def share_rows(core, full, side, first_chip, kind, keep_ref, send_ref):
    first = core == 0
    block = full.shape[0] // CHUNK_CHIPS
    full = full.reshape(CHUNK_CHIPS, block // 16, 2, 8, HEAD_DIM)
    for i in range(CHUNK_CHIPS):
        xl, low_z = divmod(first_chip + i, Y * X_HI // X_LO)
        z = low_z * 2 + side
        low = full[i, :, 0].reshape(block // 2, HEAD_DIM)
        high = full[i, :, 1].reshape(block // 2, HEAD_DIM)
        at = pl.ds(xl * (block // 2), block // 2)
        keep_ref[z, kind, at, :] = jnp.where(first, low, high).astype(jnp.bfloat16)
        send_ref[z, kind, at, :] = jnp.where(first, high, low).astype(jnp.bfloat16)


def own_half_kernel(queries, own, e_ref, att_ref, stats_ref, s_ref):
    chunks = half_chunks(own)
    top = scores_of(chunks, queries[...], s_ref)
    total, att = weights_of(chunks, top, s_ref, e_ref)
    att_ref[...] = att
    stats_ref[0:8, :] = jnp.broadcast_to(top, (8, top.shape[1]))
    stats_ref[8:16, :] = jnp.broadcast_to(total, (8, top.shape[1]))


def own_half(queries, own):
    rows = queries.shape[0]
    memory = own.shape[0] * own.shape[2]
    bf16, f32 = jnp.bfloat16, jnp.float32
    return pl.pallas_call(
        own_half_kernel,
        out_shape=(
            jax.ShapeDtypeStruct((memory, rows), bf16),
            jax.ShapeDtypeStruct((HEAD_DIM, rows), f32),
            jax.ShapeDtypeStruct((16, rows), f32),
        ),
        in_specs=[VMEM] * 2,
        out_specs=(VMEM,) * 3,
        scratch_shapes=[pltpu.VMEM((memory, rows), f32)],
        compiler_params=params(16),
        cost_estimate=pl.CostEstimate(
            flops=4 * rows * memory * HEAD_DIM,
            bytes_accessed=2 * 1024 * 1024,
            transcendentals=rows * memory,
        ),
        name="own_half",
    )(queries, own)


def both_halves_kernel(
    queries, cotangents, own, other, own_e_ref, own_att_ref, stats_ref,
    att_ref, ds_ref, keep_ref, send_ref, s_ref, e_ref,
):
    _, _, core = position()
    q = queries[...]
    chunks = half_chunks(other)
    own_top, own_total = stats_ref[0:1, :], stats_ref[8:9, :]
    top = jnp.maximum(own_top, scores_of(chunks, q, s_ref))
    total, att = weights_of(chunks, top, s_ref, e_ref)
    shrink = jnp.exp2(own_top - top)
    inverse = 1.0 / (own_total * shrink + total)
    att = (own_att_ref[...] * shrink + att) * inverse
    att_ref[...] = att.T.astype(jnp.bfloat16)
    dot = cotangents[...].astype(jnp.float32).T * inverse
    half = own_e_ref.shape[0]
    for base, source, side, weights, scaled in (
        (0, own, core, own_e_ref, dot * shrink),
        (half, other, 1 - core, e_ref, dot),
    ):
        scaled = scaled.astype(jnp.bfloat16)
        delta = jnp.sum(att * scaled.astype(jnp.float32), axis=0, keepdims=True)
        rows_scaled = scaled.T
        for rows, load, chip in half_chunks(source):
            e = weights[rows, :]
            dp = nn(load(1), scaled)
            ds = (e.astype(jnp.float32) * (dp - delta)).astype(jnp.bfloat16)
            ds_ref[pl.ds(base + rows.start, rows.size), :] = ds
            share_rows(core, nn(ds, q) * SCALE, side, chip, 0, keep_ref, send_ref)
            share_rows(core, nn(e, rows_scaled), side, chip, 1, keep_ref, send_ref)


def both_halves(queries, cotangents, own, other, own_e, own_att, stats):
    half, rows = own_e.shape
    bf16, f32 = jnp.bfloat16, jnp.float32
    parts = jax.ShapeDtypeStruct((Z, 2, 2 * half // (2 * Z), HEAD_DIM), bf16)
    return pl.pallas_call(
        both_halves_kernel,
        out_shape=(
            jax.ShapeDtypeStruct((rows, HEAD_DIM), bf16),
            jax.ShapeDtypeStruct((2 * half, rows), bf16),
            parts,
            parts,
        ),
        in_specs=[VMEM] * 7,
        out_specs=(VMEM,) * 4,
        scratch_shapes=[pltpu.VMEM((half, rows), f32), pltpu.VMEM((half, rows), bf16)],
        compiler_params=params(20),
        cost_estimate=pl.CostEstimate(
            flops=12 * rows * half * HEAD_DIM,
            bytes_accessed=4 * 1024 * 1024,
            transcendentals=rows * half,
        ),
        name="both_halves",
    )(queries, cotangents, own, other, own_e, own_att, stats)


def queries_kernel(own, other, ds_ref, att_ref, rows_out):
    rows_out[0] = att_ref[...]
    dq = 0.0
    base = 0
    for source in (own, other):
        for rows, load, _ in half_chunks(source):
            dq = dq + nn(load(0).T, ds_ref[pl.ds(base + rows.start, rows.size), :])
        base = ds_ref.shape[0] // 2
    rows_out[1] = (dq * SCALE).T.astype(jnp.bfloat16)


def queries_step(own, other, ds, att):
    memory, rows = ds.shape
    return pl.pallas_call(
        queries_kernel,
        out_shape=jax.ShapeDtypeStruct((2,) + att.shape, att.dtype),
        in_specs=[VMEM] * 4,
        out_specs=VMEM,
        compiler_params=params(12),
        cost_estimate=pl.CostEstimate(
            flops=2 * rows * memory * HEAD_DIM, bytes_accessed=2 * 1024 * 1024, transcendentals=0
        ),
        name="queries_step",
    )(own, other, ds, att)


def per_device(queries, mem_keys, mem_values, grad_out):
    q_came = trade(queries)
    grad_out, q_came = lax.optimization_barrier((grad_out, q_came))
    q, do = select(queries, grad_out, q_came, trade(grad_out))
    own = exchange(pack(mem_keys, mem_values), head_groups())
    own, q, do = lax.optimization_barrier((own, q, do))
    other = permute(own, other_core)
    att, ds, keep, send = both_halves(q, do, own, other, *own_half(q, own))
    came = permute(send, other_core)
    rows = queries_step(own, other, ds, att)
    traded = trade(rows)
    sums = sum_over_z(keep, came)
    attended, query_gradients = unpack(rows, traded)
    grad_keys, grad_values = columns(exchange(sums, column_groups()))
    return attended, query_gradients, grad_keys, grad_values


def solution(mesh):
    in_specs = (P("query", "head"), P("head", None), P("head", None), P("query", "head"))
    out_specs = (
        P("query", "head"),
        P("query", "head"),
        P(("query", "head"), None),
        P(("query", "head"), None),
    )
    return jax.shard_map(
        per_device, mesh=mesh, in_specs=in_specs, out_specs=out_specs, check_vma=False
    )
```

```python
import functools
import itertools

import jax
import jax.numpy as jnp
from jax import lax
from jax.experimental import pallas as pl
from jax.experimental.pallas import tpu as pltpu
from jax.sharding import PartitionSpec as P

HEAD_DIM = 256
AXES = ("query", "head")
X_LO, Z, Y, X_HI, CORE = 2, 8, 4, 2, 2
SCALE = HEAD_DIM ** (-0.5)
CHUNK_CHIPS = 8
LOG2E = 1.4426950408889634


def position():
    query, head = lax.axis_index("query"), lax.axis_index("head")
    return lax.div(query, Z), lax.rem(query, Z), lax.rem(head, CORE)


def device(xl, z, y, xh, c):
    return (xl * Z + z) * (Y * X_HI * CORE) + (y * X_HI + xh) * CORE + c


def permute(array, to):
    pairs = [
        (device(*at), device(*to(*at)))
        for at in itertools.product(range(X_LO), range(Z), range(Y), range(X_HI), range(CORE))
    ]
    return lax.ppermute(array, AXES, pairs)


def exchange(array, groups):
    return lax.all_to_all(
        array, AXES, split_axis=0, concat_axis=0, axis_index_groups=groups, tiled=True
    )


def trade(array):
    pairs = []
    for z, y, xh in itertools.product(range(Z), range(Y), range(X_HI)):
        one, two = device(0, z, y, xh, 1), device(1, z, y, xh, 0)
        pairs += [(one, two), (two, one)]
    return lax.ppermute(array, AXES, pairs)


def trade_in_two(array):
    over, home = [], []
    for z, y, xh in itertools.product(range(Z), range(Y), range(X_HI)):
        for xl in range(X_LO):
            middle = device(1 - xl, z, y, xh, 1 - xl)
            over.append((device(xl, z, y, xh, 1 - xl), middle))
            home.append((middle, device(1 - xl, z, y, xh, xl)))
    return lax.ppermute(lax.ppermute(array, AXES, over), AXES, home)


def other_core(xl, z, y, xh, c):
    return (xl, z, y, xh, 1 - c)


def head_groups():
    return [
        [device(xl, z, y, xh, c) for y in range(Y) for xh in range(X_HI)]
        for xl in range(X_LO)
        for z in range(Z)
        for c in range(CORE)
    ]


def column_groups():
    return [
        [device(xl, z, y, xh, c) for y in range(Y) for xh in range(X_HI) for xl in range(X_LO)]
        for z in range(Z)
        for c in range(CORE)
    ]


VMEM = pl.BlockSpec(memory_space=pltpu.VMEM)
ANY = pl.BlockSpec(memory_space=pl.ANY)


def params(mib):
    return pltpu.CompilerParams(vmem_limit_bytes=mib * 1024 * 1024)


def pack_kernel(keys, values, out, held, sems):
    xl, _, _ = position()
    copies = [
        pltpu.make_async_copy(source, held.at[kind], sems.at[kind])
        for kind, source in enumerate((keys, values))
    ]
    for copy in copies:
        copy.start()
    for kind, copy in enumerate(copies):
        copy.wait()
        for chip in range(Y * X_HI):
            start = pl.multiple_of((chip * 2 + xl) * HEAD_DIM, HEAD_DIM)
            out[chip, kind] = held[kind, :, pl.ds(start, HEAD_DIM)]


def pack(keys, values):
    shape = (Y * X_HI, 2, keys.shape[0], HEAD_DIM)
    return pl.pallas_call(
        pack_kernel,
        out_shape=jax.ShapeDtypeStruct(shape, keys.dtype),
        in_specs=[ANY, ANY],
        out_specs=VMEM,
        scratch_shapes=[
            pltpu.VMEM((2,) + keys.shape, keys.dtype),
            pltpu.SemaphoreType.DMA((2,)),
        ],
        compiler_params=params(56),
        name="pack",
    )(keys, values)


def select_kernel(queries, cotangents, q_came, do_came, q, do):
    xl, _, core = position()
    stay = xl == core
    q[...] = jnp.where(stay, queries[...], q_came[...])
    do[...] = jnp.where(stay, cotangents[...], do_came[...])


def select(queries, cotangents, q_came, do_came):
    out = jax.ShapeDtypeStruct(queries.shape, queries.dtype)
    return pl.pallas_call(
        select_kernel,
        out_shape=(out, out),
        in_specs=[VMEM] * 4,
        out_specs=(VMEM, VMEM),
        input_output_aliases={2: 0, 3: 1},
        compiler_params=params(8),
        cost_estimate=pl.CostEstimate(flops=0, bytes_accessed=3 * 1024 * 1024, transcendentals=0),
        name="select",
    )(queries, cotangents, q_came, do_came)


def unpack_kernel(mine, came, attended, gradients):
    xl, _, core = position()
    stay = xl == core
    attended[...] = jnp.where(stay, mine[0], came[0])
    gradients[...] = jnp.where(stay, mine[1], came[1])


def unpack(mine, came):
    out = jax.ShapeDtypeStruct(mine.shape[1:], mine.dtype)
    return pl.pallas_call(
        unpack_kernel,
        out_shape=(out, out),
        in_specs=[VMEM, VMEM],
        out_specs=(VMEM, VMEM),
        compiler_params=params(12),
        name="unpack",
    )(mine, came)


def core_sum_kernel(keep, came, up, down, across, ahead, behind, own):
    _, z, _ = position()

    def chunk(distance):
        at = lax.rem(z + distance, Z)
        return keep[at].astype(jnp.float32) + came[at].astype(jnp.float32)

    bf16 = jnp.bfloat16
    up[0] = chunk(3).astype(bf16)
    up[1] = chunk(1).astype(bf16)
    down[0] = chunk(5).astype(bf16)
    down[1] = chunk(7).astype(bf16)
    across[...] = chunk(4).astype(bf16)
    ahead[...] = chunk(2)
    behind[...] = chunk(6)
    own[...] = chunk(0)


def core_sum(keep, came):
    shape = keep.shape[1:]
    bf16, f32 = jnp.bfloat16, jnp.float32
    return pl.pallas_call(
        core_sum_kernel,
        out_shape=(
            jax.ShapeDtypeStruct((2,) + shape, bf16),
            jax.ShapeDtypeStruct((2,) + shape, bf16),
            jax.ShapeDtypeStruct(shape, bf16),
            jax.ShapeDtypeStruct(shape, f32),
            jax.ShapeDtypeStruct(shape, f32),
            jax.ShapeDtypeStruct(shape, f32),
        ),
        in_specs=[VMEM, VMEM],
        out_specs=(VMEM,) * 6,
        compiler_params=params(12),
        name="core_sum",
    )(keep, came)


def middle_sum_kernel(ahead, behind, from_below, from_above, across, up, down):
    far = across[...].astype(jnp.float32)
    first = position()[2] == 0
    zero = jnp.zeros_like(far)
    below = from_below[0].astype(jnp.float32) + jnp.where(first, far, zero)
    above = from_above[0].astype(jnp.float32) + jnp.where(first, zero, far)
    up[...] = (ahead[...] + below).astype(jnp.bfloat16)
    down[...] = (behind[...] + above).astype(jnp.bfloat16)


def middle_sum(ahead, behind, from_below, from_above, across):
    out = jax.ShapeDtypeStruct(ahead.shape, jnp.bfloat16)
    return pl.pallas_call(
        middle_sum_kernel,
        out_shape=(out, out),
        in_specs=[VMEM] * 5,
        out_specs=(VMEM, VMEM),
        compiler_params=params(12),
        name="middle_sum",
    )(ahead, behind, from_below, from_above, across)


def last_sum_kernel(own, from_below, from_above, low, high, out):
    f32 = jnp.float32
    total = own[...] + from_below[1].astype(f32) + from_above[1].astype(f32)
    total = total + low[...].astype(f32) + high[...].astype(f32)
    total = total.reshape(2, X_LO, Y * X_HI, 8, HEAD_DIM)
    for xl in range(X_LO):
        for chip in range(Y * X_HI):
            both = jnp.concatenate([total[0, xl, chip], total[1, xl, chip]], axis=0)
            out[chip * 2 + xl] = both.astype(jnp.bfloat16)


def last_sum(own, from_below, from_above, low, high):
    return pl.pallas_call(
        last_sum_kernel,
        out_shape=jax.ShapeDtypeStruct((Y * X_HI * X_LO, 16, HEAD_DIM), jnp.bfloat16),
        in_specs=[VMEM] * 5,
        out_specs=VMEM,
        compiler_params=params(12),
        name="last_sum",
    )(own, from_below, from_above, low, high)


def columns_kernel(parts, keys, values):
    for head in range(Y * X_HI * X_LO):
        both = parts[head].astype(jnp.float32)
        at = pl.ds(head * HEAD_DIM, HEAD_DIM)
        keys[:, at] = both[:8].astype(jnp.bfloat16)
        values[:, at] = both[8:].astype(jnp.bfloat16)


def columns(parts):
    out = jax.ShapeDtypeStruct((8, parts.shape[0] * HEAD_DIM), jnp.bfloat16)
    return pl.pallas_call(
        columns_kernel,
        out_shape=(out, out),
        in_specs=[VMEM],
        out_specs=(VMEM, VMEM),
        compiler_params=params(12),
        name="columns",
    )(parts)


def sum_over_z(keep, came):
    above = lambda hops: lambda xl, z, y, xh, c: (xl, (z + hops) % Z, y, xh, c)
    over = lambda xl, z, y, xh, c: (xl, (z + (2 if c == 0 else 6)) % Z, y, xh, c)
    up, down, across, ahead, behind, own = core_sum(keep, came)
    from_below = permute(up, above(1))
    from_above = permute(down, above(7))
    far = permute(across, over)
    up, down = middle_sum(ahead, behind, from_below, from_above, far)
    low = permute(up, above(2))
    high = permute(down, above(6))
    return last_sum(own, from_below, from_above, low, high)


def nt(a, b):
    return lax.dot_general(a, b, (((1,), (1,)), ((), ())), preferred_element_type=jnp.float32)


def nn(a, b):
    return jnp.dot(a, b, preferred_element_type=jnp.float32)


def half_chunks(source):
    size = CHUNK_CHIPS * source.shape[2]
    found = []
    for chip in range(0, Y * X_HI, CHUNK_CHIPS):
        load = lambda kind, chip=chip: source[chip : chip + CHUNK_CHIPS, kind].reshape(
            size, HEAD_DIM
        )
        found.append((pl.ds(len(found) * size, size), load, chip))
    return found


def scores_of(chunks, q, s_ref):
    top = None
    for rows, load, _ in chunks:
        s = nt(load(0), q)
        s_ref[rows, :] = s
        here = jnp.max(s, axis=0, keepdims=True)
        top = here if top is None else jnp.maximum(top, here)
    return top * (LOG2E * SCALE)


def weights_of(chunks, top, s_ref, e_ref):
    total, att = 0.0, 0.0
    for rows, load, _ in chunks:
        e = jnp.exp2(s_ref[rows, :] * (LOG2E * SCALE) - top)
        total = total + jnp.sum(e, axis=0, keepdims=True)
        eb = e.astype(jnp.bfloat16)
        e_ref[rows, :] = eb
        att = att + nn(load(1).T, eb)
    return total, att


def share_rows(core, full, side, first_chip, kind, keep_ref, send_ref):
    first = core == 0
    block = full.shape[0] // CHUNK_CHIPS
    full = full.reshape(CHUNK_CHIPS, block // 16, 2, 8, HEAD_DIM)
    for i in range(CHUNK_CHIPS):
        xl, low_z = divmod(first_chip + i, Y * X_HI // X_LO)
        z = low_z * 2 + side
        low = full[i, :, 0].reshape(block // 2, HEAD_DIM)
        high = full[i, :, 1].reshape(block // 2, HEAD_DIM)
        at = pl.ds(xl * (block // 2), block // 2)
        keep_ref[z, kind, at, :] = jnp.where(first, low, high).astype(jnp.bfloat16)
        send_ref[z, kind, at, :] = jnp.where(first, high, low).astype(jnp.bfloat16)


def own_half_kernel(queries, own, e_ref, att_ref, stats_ref, s_ref):
    chunks = half_chunks(own)
    top = scores_of(chunks, queries[...], s_ref)
    total, att = weights_of(chunks, top, s_ref, e_ref)
    att_ref[...] = att
    stats_ref[0:8, :] = jnp.broadcast_to(top, (8, top.shape[1]))
    stats_ref[8:16, :] = jnp.broadcast_to(total, (8, top.shape[1]))


def own_half(queries, own):
    rows = queries.shape[0]
    memory = own.shape[0] * own.shape[2]
    bf16, f32 = jnp.bfloat16, jnp.float32
    return pl.pallas_call(
        own_half_kernel,
        out_shape=(
            jax.ShapeDtypeStruct((memory, rows), bf16),
            jax.ShapeDtypeStruct((HEAD_DIM, rows), f32),
            jax.ShapeDtypeStruct((16, rows), f32),
        ),
        in_specs=[VMEM] * 2,
        out_specs=(VMEM,) * 3,
        scratch_shapes=[pltpu.VMEM((memory, rows), f32)],
        compiler_params=params(16),
        cost_estimate=pl.CostEstimate(
            flops=4 * rows * memory * HEAD_DIM,
            bytes_accessed=2 * 1024 * 1024,
            transcendentals=rows * memory,
        ),
        name="own_half",
    )(queries, own)


def both_halves_kernel(
    queries, cotangents, own, other, own_e_ref, own_att_ref, stats_ref,
    att_ref, ds_ref, keep_ref, send_ref, s_ref, e_ref,
):
    _, _, core = position()
    q = queries[...]
    chunks = half_chunks(other)
    own_top, own_total = stats_ref[0:1, :], stats_ref[8:9, :]
    top = jnp.maximum(own_top, scores_of(chunks, q, s_ref))
    total, att = weights_of(chunks, top, s_ref, e_ref)
    shrink = jnp.exp2(own_top - top)
    inverse = 1.0 / (own_total * shrink + total)
    att = (own_att_ref[...] * shrink + att) * inverse
    att_ref[...] = att.T.astype(jnp.bfloat16)
    dot = cotangents[...].astype(jnp.float32).T * inverse
    half = own_e_ref.shape[0]
    for base, source, side, weights, scaled in (
        (0, own, core, own_e_ref, dot * shrink),
        (half, other, 1 - core, e_ref, dot),
    ):
        scaled = scaled.astype(jnp.bfloat16)
        delta = jnp.sum(att * scaled.astype(jnp.float32), axis=0, keepdims=True)
        rows_scaled = scaled.T
        for rows, load, chip in half_chunks(source):
            e = weights[rows, :]
            dp = nn(load(1), scaled)
            ds = (e.astype(jnp.float32) * (dp - delta)).astype(jnp.bfloat16)
            ds_ref[pl.ds(base + rows.start, rows.size), :] = ds
            share_rows(core, nn(ds, q) * SCALE, side, chip, 0, keep_ref, send_ref)
            share_rows(core, nn(e, rows_scaled), side, chip, 1, keep_ref, send_ref)


def both_halves(queries, cotangents, own, other, own_e, own_att, stats):
    half, rows = own_e.shape
    bf16, f32 = jnp.bfloat16, jnp.float32
    parts = jax.ShapeDtypeStruct((Z, 2, 2 * half // (2 * Z), HEAD_DIM), bf16)
    return pl.pallas_call(
        both_halves_kernel,
        out_shape=(
            jax.ShapeDtypeStruct((rows, HEAD_DIM), bf16),
            jax.ShapeDtypeStruct((2 * half, rows), bf16),
            parts,
            parts,
        ),
        in_specs=[VMEM] * 7,
        out_specs=(VMEM,) * 4,
        scratch_shapes=[pltpu.VMEM((half, rows), f32), pltpu.VMEM((half, rows), bf16)],
        compiler_params=params(20),
        cost_estimate=pl.CostEstimate(
            flops=12 * rows * half * HEAD_DIM,
            bytes_accessed=4 * 1024 * 1024,
            transcendentals=rows * half,
        ),
        name="both_halves",
    )(queries, cotangents, own, other, own_e, own_att, stats)


def queries_kernel(own, other, ds_ref, att_ref, rows_out):
    rows_out[0] = att_ref[...]
    dq = 0.0
    base = 0
    for source in (own, other):
        for rows, load, _ in half_chunks(source):
            dq = dq + nn(load(0).T, ds_ref[pl.ds(base + rows.start, rows.size), :])
        base = ds_ref.shape[0] // 2
    rows_out[1] = (dq * SCALE).T.astype(jnp.bfloat16)


def queries_step(own, other, ds, att):
    memory, rows = ds.shape
    return pl.pallas_call(
        queries_kernel,
        out_shape=jax.ShapeDtypeStruct((2,) + att.shape, att.dtype),
        in_specs=[VMEM] * 4,
        out_specs=VMEM,
        compiler_params=params(12),
        cost_estimate=pl.CostEstimate(
            flops=2 * rows * memory * HEAD_DIM, bytes_accessed=2 * 1024 * 1024, transcendentals=0
        ),
        name="queries_step",
    )(own, other, ds, att)


def per_device(queries, mem_keys, mem_values, grad_out):
    q, do = select(queries, grad_out, trade_in_two(queries), trade_in_two(grad_out))
    own = exchange(pack(mem_keys, mem_values), head_groups())
    own, q, do = lax.optimization_barrier((own, q, do))
    other = permute(own, other_core)
    att, ds, keep, send = both_halves(q, do, own, other, *own_half(q, own))
    came = permute(send, other_core)
    rows = queries_step(own, other, ds, att)
    traded = trade(rows)
    sums = sum_over_z(keep, came)
    attended, query_gradients = unpack(rows, traded)
    grad_keys, grad_values = columns(exchange(sums, column_groups()))
    return attended, query_gradients, grad_keys, grad_values


def solution(mesh):
    in_specs = (P("query", "head"), P("head", None), P("head", None), P("query", "head"))
    out_specs = (
        P("query", "head"),
        P("query", "head"),
        P(("query", "head"), None),
        P(("query", "head"), None),
    )
    return jax.shard_map(
        per_device, mesh=mesh, in_specs=in_specs, out_specs=out_specs, check_vma=False
    )
```

```python
import functools
import itertools

import jax
import jax.numpy as jnp
from jax import lax
from jax.experimental import pallas as pl
from jax.experimental.pallas import tpu as pltpu
from jax.sharding import PartitionSpec as P

HEAD_DIM = 256
AXES = ("query", "head")
X_LO, Z, Y, X_HI, CORE = 2, 8, 4, 2, 2
SCALE = HEAD_DIM ** (-0.5)
CHUNK_CHIPS = 8
LOG2E = 1.4426950408889634


def position():
    query, head = lax.axis_index("query"), lax.axis_index("head")
    return lax.div(query, Z), lax.rem(query, Z), lax.rem(head, CORE)


def device(xl, z, y, xh, c):
    return (xl * Z + z) * (Y * X_HI * CORE) + (y * X_HI + xh) * CORE + c


def permute(array, to):
    pairs = [
        (device(*at), device(*to(*at)))
        for at in itertools.product(range(X_LO), range(Z), range(Y), range(X_HI), range(CORE))
    ]
    return lax.ppermute(array, AXES, pairs)


def exchange(array, groups):
    return lax.all_to_all(
        array, AXES, split_axis=0, concat_axis=0, axis_index_groups=groups, tiled=True
    )


def trade(array):
    pairs = []
    for z, y, xh in itertools.product(range(Z), range(Y), range(X_HI)):
        one, two = device(0, z, y, xh, 1), device(1, z, y, xh, 0)
        pairs += [(one, two), (two, one)]
    return lax.ppermute(array, AXES, pairs)


def trade_in_two(array):
    over, home = [], []
    for z, y, xh in itertools.product(range(Z), range(Y), range(X_HI)):
        for xl in range(X_LO):
            middle = device(1 - xl, z, y, xh, 1 - xl)
            over.append((device(xl, z, y, xh, 1 - xl), middle))
            over.append((device(xl, z, y, xh, xl), device(xl, z, y, xh, 1 - xl)))
            home.append((middle, device(1 - xl, z, y, xh, xl)))
    return lax.ppermute(lax.ppermute(array, AXES, over), AXES, home)


def other_core(xl, z, y, xh, c):
    return (xl, z, y, xh, 1 - c)


def head_groups():
    return [
        [device(xl, z, y, xh, c) for y in range(Y) for xh in range(X_HI)]
        for xl in range(X_LO)
        for z in range(Z)
        for c in range(CORE)
    ]


def column_groups():
    return [
        [device(xl, z, y, xh, c) for y in range(Y) for xh in range(X_HI) for xl in range(X_LO)]
        for z in range(Z)
        for c in range(CORE)
    ]


VMEM = pl.BlockSpec(memory_space=pltpu.VMEM)
ANY = pl.BlockSpec(memory_space=pl.ANY)


def params(mib):
    return pltpu.CompilerParams(vmem_limit_bytes=mib * 1024 * 1024)


def pack_kernel(keys, values, out, held, packed, sems):
    xl, _, _ = position()
    half = keys.shape[0] // 2
    pieces = [(kind, pl.ds(i * half, half)) for kind in range(2) for i in range(2)]
    loads, stores = [], []
    for at, (kind, rows) in enumerate(pieces):
        source = (keys, values)[kind].at[rows]
        loads.append(pltpu.make_async_copy(source, held.at[kind, rows], sems.at[0, at]))
        stores.append(
            pltpu.make_async_copy(packed.at[:, kind, rows], out.at[:, kind, rows], sems.at[1, at])
        )
        loads[at].start()
    for at, (kind, rows) in enumerate(pieces):
        loads[at].wait()
        for chip in range(Y * X_HI):
            start = pl.multiple_of((chip * 2 + xl) * HEAD_DIM, HEAD_DIM)
            packed[chip, kind, rows] = held[kind, rows, pl.ds(start, HEAD_DIM)]
        stores[at].start()
    for store in stores:
        store.wait()


def pack(keys, values):
    shape = (Y * X_HI, 2, keys.shape[0], HEAD_DIM)
    return pl.pallas_call(
        pack_kernel,
        out_shape=jax.ShapeDtypeStruct(shape, keys.dtype),
        in_specs=[ANY, ANY],
        out_specs=ANY,
        scratch_shapes=[
            pltpu.VMEM((2,) + keys.shape, keys.dtype),
            pltpu.VMEM(shape, keys.dtype),
            pltpu.SemaphoreType.DMA((2, 4)),
        ],
        compiler_params=params(56),
        name="pack",
    )(keys, values)


def select_kernel(queries, cotangents, q_came, do_came, q, do):
    xl, _, core = position()
    stay = xl == core
    q[...] = jnp.where(stay, queries[...], q_came[...])
    do[...] = jnp.where(stay, cotangents[...], do_came[...])


def select(queries, cotangents, q_came, do_came):
    out = jax.ShapeDtypeStruct(queries.shape, queries.dtype)
    return pl.pallas_call(
        select_kernel,
        out_shape=(out, out),
        in_specs=[VMEM] * 4,
        out_specs=(VMEM, VMEM),
        input_output_aliases={2: 0, 3: 1},
        compiler_params=params(8),
        cost_estimate=pl.CostEstimate(flops=0, bytes_accessed=3 * 1024 * 1024, transcendentals=0),
        name="select",
    )(queries, cotangents, q_came, do_came)


def unpack_kernel(mine, came, attended, gradients):
    xl, _, core = position()
    stay = xl == core
    attended[...] = jnp.where(stay, mine[0], came[0])
    gradients[...] = jnp.where(stay, mine[1], came[1])


def unpack(mine, came):
    out = jax.ShapeDtypeStruct(mine.shape[1:], mine.dtype)
    return pl.pallas_call(
        unpack_kernel,
        out_shape=(out, out),
        in_specs=[VMEM, VMEM],
        out_specs=(VMEM, VMEM),
        compiler_params=params(12),
        name="unpack",
    )(mine, came)


def core_sum_kernel(keep, came, up, down, across, ahead, behind, own):
    _, z, _ = position()

    def chunk(distance):
        at = lax.rem(z + distance, Z)
        return keep[at].astype(jnp.float32) + came[at].astype(jnp.float32)

    bf16 = jnp.bfloat16
    up[0] = chunk(3).astype(bf16)
    up[1] = chunk(1).astype(bf16)
    down[0] = chunk(5).astype(bf16)
    down[1] = chunk(7).astype(bf16)
    across[...] = chunk(4).astype(bf16)
    ahead[...] = chunk(2)
    behind[...] = chunk(6)
    own[...] = chunk(0)


def core_sum(keep, came):
    shape = keep.shape[1:]
    bf16, f32 = jnp.bfloat16, jnp.float32
    return pl.pallas_call(
        core_sum_kernel,
        out_shape=(
            jax.ShapeDtypeStruct((2,) + shape, bf16),
            jax.ShapeDtypeStruct((2,) + shape, bf16),
            jax.ShapeDtypeStruct(shape, bf16),
            jax.ShapeDtypeStruct(shape, f32),
            jax.ShapeDtypeStruct(shape, f32),
            jax.ShapeDtypeStruct(shape, f32),
        ),
        in_specs=[VMEM, VMEM],
        out_specs=(VMEM,) * 6,
        compiler_params=params(12),
        name="core_sum",
    )(keep, came)


def middle_sum_kernel(ahead, behind, from_below, from_above, across, up, down):
    far = across[...].astype(jnp.float32)
    first = position()[2] == 0
    zero = jnp.zeros_like(far)
    below = from_below[0].astype(jnp.float32) + jnp.where(first, far, zero)
    above = from_above[0].astype(jnp.float32) + jnp.where(first, zero, far)
    up[...] = (ahead[...] + below).astype(jnp.bfloat16)
    down[...] = (behind[...] + above).astype(jnp.bfloat16)


def middle_sum(ahead, behind, from_below, from_above, across):
    out = jax.ShapeDtypeStruct(ahead.shape, jnp.bfloat16)
    return pl.pallas_call(
        middle_sum_kernel,
        out_shape=(out, out),
        in_specs=[VMEM] * 5,
        out_specs=(VMEM, VMEM),
        compiler_params=params(12),
        name="middle_sum",
    )(ahead, behind, from_below, from_above, across)


def last_sum_kernel(own, from_below, from_above, low, high, out):
    f32 = jnp.float32
    total = own[...] + from_below[1].astype(f32) + from_above[1].astype(f32)
    total = total + low[...].astype(f32) + high[...].astype(f32)
    total = total.reshape(2, X_LO, Y * X_HI, 8, HEAD_DIM)
    for xl in range(X_LO):
        for chip in range(Y * X_HI):
            both = jnp.concatenate([total[0, xl, chip], total[1, xl, chip]], axis=0)
            out[chip * 2 + xl] = both.astype(jnp.bfloat16)


def last_sum(own, from_below, from_above, low, high):
    return pl.pallas_call(
        last_sum_kernel,
        out_shape=jax.ShapeDtypeStruct((Y * X_HI * X_LO, 16, HEAD_DIM), jnp.bfloat16),
        in_specs=[VMEM] * 5,
        out_specs=VMEM,
        compiler_params=params(12),
        name="last_sum",
    )(own, from_below, from_above, low, high)


def columns_kernel(parts, keys, values):
    for head in range(Y * X_HI * X_LO):
        both = parts[head].astype(jnp.float32)
        at = pl.ds(head * HEAD_DIM, HEAD_DIM)
        keys[:, at] = both[:8].astype(jnp.bfloat16)
        values[:, at] = both[8:].astype(jnp.bfloat16)


def columns(parts):
    out = jax.ShapeDtypeStruct((8, parts.shape[0] * HEAD_DIM), jnp.bfloat16)
    return pl.pallas_call(
        columns_kernel,
        out_shape=(out, out),
        in_specs=[VMEM],
        out_specs=(VMEM, VMEM),
        compiler_params=params(12),
        name="columns",
    )(parts)


def sum_over_z(keep, came):
    above = lambda hops: lambda xl, z, y, xh, c: (xl, (z + hops) % Z, y, xh, c)
    over = lambda xl, z, y, xh, c: (xl, (z + (2 if c == 0 else 6)) % Z, y, xh, c)
    up, down, across, ahead, behind, own = core_sum(keep, came)
    from_below = permute(up, above(1))
    from_above = permute(down, above(7))
    far = permute(across, over)
    up, down = middle_sum(ahead, behind, from_below, from_above, far)
    low = permute(up, above(2))
    high = permute(down, above(6))
    return last_sum(own, from_below, from_above, low, high)


def nt(a, b):
    return lax.dot_general(a, b, (((1,), (1,)), ((), ())), preferred_element_type=jnp.float32)


def nn(a, b):
    return jnp.dot(a, b, preferred_element_type=jnp.float32)


def half_chunks(source):
    size = CHUNK_CHIPS * source.shape[2]
    found = []
    for chip in range(0, Y * X_HI, CHUNK_CHIPS):
        load = lambda kind, chip=chip: source[chip : chip + CHUNK_CHIPS, kind].reshape(
            size, HEAD_DIM
        )
        found.append((pl.ds(len(found) * size, size), load, chip))
    return found


def scores_of(chunks, q, s_ref):
    top = None
    for rows, load, _ in chunks:
        s = nt(load(0), q)
        s_ref[rows, :] = s
        here = jnp.max(s, axis=0, keepdims=True)
        top = here if top is None else jnp.maximum(top, here)
    return top * (LOG2E * SCALE)


def weights_of(chunks, top, s_ref, e_ref):
    total, att = 0.0, 0.0
    for rows, load, _ in chunks:
        e = jnp.exp2(s_ref[rows, :] * (LOG2E * SCALE) - top)
        total = total + jnp.sum(e, axis=0, keepdims=True)
        eb = e.astype(jnp.bfloat16)
        e_ref[rows, :] = eb
        att = att + nn(load(1).T, eb)
    return total, att


def share_rows(core, full, side, first_chip, kind, keep_ref, send_ref):
    first = core == 0
    block = full.shape[0] // CHUNK_CHIPS
    full = full.reshape(CHUNK_CHIPS, block // 16, 2, 8, HEAD_DIM)
    for i in range(CHUNK_CHIPS):
        xl, low_z = divmod(first_chip + i, Y * X_HI // X_LO)
        z = low_z * 2 + side
        low = full[i, :, 0].reshape(block // 2, HEAD_DIM)
        high = full[i, :, 1].reshape(block // 2, HEAD_DIM)
        at = pl.ds(xl * (block // 2), block // 2)
        keep_ref[z, kind, at, :] = jnp.where(first, low, high).astype(jnp.bfloat16)
        send_ref[z, kind, at, :] = jnp.where(first, high, low).astype(jnp.bfloat16)


def own_half_kernel(queries, own, e_ref, att_ref, stats_ref, s_ref):
    chunks = half_chunks(own)
    top = scores_of(chunks, queries[...], s_ref)
    total, att = weights_of(chunks, top, s_ref, e_ref)
    att_ref[...] = att
    stats_ref[0:8, :] = jnp.broadcast_to(top, (8, top.shape[1]))
    stats_ref[8:16, :] = jnp.broadcast_to(total, (8, top.shape[1]))


def own_half(queries, own):
    rows = queries.shape[0]
    memory = own.shape[0] * own.shape[2]
    bf16, f32 = jnp.bfloat16, jnp.float32
    return pl.pallas_call(
        own_half_kernel,
        out_shape=(
            jax.ShapeDtypeStruct((memory, rows), bf16),
            jax.ShapeDtypeStruct((HEAD_DIM, rows), f32),
            jax.ShapeDtypeStruct((16, rows), f32),
        ),
        in_specs=[VMEM] * 2,
        out_specs=(VMEM,) * 3,
        scratch_shapes=[pltpu.VMEM((memory, rows), f32)],
        compiler_params=params(16),
        cost_estimate=pl.CostEstimate(
            flops=4 * rows * memory * HEAD_DIM,
            bytes_accessed=2 * 1024 * 1024,
            transcendentals=rows * memory,
        ),
        name="own_half",
    )(queries, own)


def both_halves_kernel(
    queries, cotangents, own, other, own_e_ref, own_att_ref, stats_ref,
    att_ref, ds_ref, keep_ref, send_ref, s_ref, e_ref,
):
    _, _, core = position()
    q = queries[...]
    chunks = half_chunks(other)
    own_top, own_total = stats_ref[0:1, :], stats_ref[8:9, :]
    top = jnp.maximum(own_top, scores_of(chunks, q, s_ref))
    total, att = weights_of(chunks, top, s_ref, e_ref)
    shrink = jnp.exp2(own_top - top)
    inverse = 1.0 / (own_total * shrink + total)
    att = (own_att_ref[...] * shrink + att) * inverse
    att_ref[...] = att.T.astype(jnp.bfloat16)
    dot = cotangents[...].astype(jnp.float32).T * inverse
    half = own_e_ref.shape[0]
    for base, source, side, weights, scaled in (
        (0, own, core, own_e_ref, dot * shrink),
        (half, other, 1 - core, e_ref, dot),
    ):
        scaled = scaled.astype(jnp.bfloat16)
        delta = jnp.sum(att * scaled.astype(jnp.float32), axis=0, keepdims=True)
        rows_scaled = scaled.T
        for rows, load, chip in half_chunks(source):
            e = weights[rows, :]
            dp = nn(load(1), scaled)
            ds = (e.astype(jnp.float32) * (dp - delta)).astype(jnp.bfloat16)
            ds_ref[pl.ds(base + rows.start, rows.size), :] = ds
            share_rows(core, nn(ds, q) * SCALE, side, chip, 0, keep_ref, send_ref)
            share_rows(core, nn(e, rows_scaled), side, chip, 1, keep_ref, send_ref)


def both_halves(queries, cotangents, own, other, own_e, own_att, stats):
    half, rows = own_e.shape
    bf16, f32 = jnp.bfloat16, jnp.float32
    parts = jax.ShapeDtypeStruct((Z, 2, 2 * half // (2 * Z), HEAD_DIM), bf16)
    return pl.pallas_call(
        both_halves_kernel,
        out_shape=(
            jax.ShapeDtypeStruct((rows, HEAD_DIM), bf16),
            jax.ShapeDtypeStruct((2 * half, rows), bf16),
            parts,
            parts,
        ),
        in_specs=[VMEM] * 7,
        out_specs=(VMEM,) * 4,
        scratch_shapes=[pltpu.VMEM((half, rows), f32), pltpu.VMEM((half, rows), bf16)],
        compiler_params=params(20),
        cost_estimate=pl.CostEstimate(
            flops=12 * rows * half * HEAD_DIM,
            bytes_accessed=4 * 1024 * 1024,
            transcendentals=rows * half,
        ),
        name="both_halves",
    )(queries, cotangents, own, other, own_e, own_att, stats)


def queries_kernel(own, other, ds_ref, att_ref, rows_out):
    rows_out[0] = att_ref[...]
    dq = 0.0
    base = 0
    for source in (own, other):
        for rows, load, _ in half_chunks(source):
            dq = dq + nn(load(0).T, ds_ref[pl.ds(base + rows.start, rows.size), :])
        base = ds_ref.shape[0] // 2
    rows_out[1] = (dq * SCALE).T.astype(jnp.bfloat16)


def queries_step(own, other, ds, att):
    memory, rows = ds.shape
    return pl.pallas_call(
        queries_kernel,
        out_shape=jax.ShapeDtypeStruct((2,) + att.shape, att.dtype),
        in_specs=[VMEM] * 4,
        out_specs=VMEM,
        compiler_params=params(12),
        cost_estimate=pl.CostEstimate(
            flops=2 * rows * memory * HEAD_DIM, bytes_accessed=2 * 1024 * 1024, transcendentals=0
        ),
        name="queries_step",
    )(own, other, ds, att)


def per_device(queries, mem_keys, mem_values, grad_out):
    q, do = select(queries, grad_out, trade_in_two(queries), trade_in_two(grad_out))
    own = exchange(pack(mem_keys, mem_values), head_groups())
    own, q, do = lax.optimization_barrier((own, q, do))
    other = permute(own, other_core)
    att, ds, keep, send = both_halves(q, do, own, other, *own_half(q, own))
    came = permute(send, other_core)
    rows = queries_step(own, other, ds, att)
    traded = trade(rows)
    sums = sum_over_z(keep, came)
    attended, query_gradients = unpack(rows, traded)
    grad_keys, grad_values = columns(exchange(sums, column_groups()))
    return attended, query_gradients, grad_keys, grad_values


def solution(mesh):
    in_specs = (P("query", "head"), P("head", None), P("head", None), P("query", "head"))
    out_specs = (
        P("query", "head"),
        P("query", "head"),
        P(("query", "head"), None),
        P(("query", "head"), None),
    )
    return jax.shard_map(
        per_device, mesh=mesh, in_specs=in_specs, out_specs=out_specs, check_vma=False
    )
```

```python
import functools
import itertools

import jax
import jax.numpy as jnp
from jax import lax
from jax.experimental import pallas as pl
from jax.experimental.pallas import tpu as pltpu
from jax.sharding import PartitionSpec as P

HEAD_DIM = 256
AXES = ("query", "head")
X_LO, Z, Y, X_HI, CORE = 2, 8, 4, 2, 2
SCALE = HEAD_DIM ** (-0.5)
CHUNK_CHIPS = 8
LOG2E = 1.4426950408889634


def position():
    query, head = lax.axis_index("query"), lax.axis_index("head")
    return lax.div(query, Z), lax.rem(query, Z), lax.rem(head, CORE)


def device(xl, z, y, xh, c):
    return (xl * Z + z) * (Y * X_HI * CORE) + (y * X_HI + xh) * CORE + c


def permute(array, to):
    pairs = [
        (device(*at), device(*to(*at)))
        for at in itertools.product(range(X_LO), range(Z), range(Y), range(X_HI), range(CORE))
    ]
    return lax.ppermute(array, AXES, pairs)


def exchange(array, groups):
    return lax.all_to_all(
        array, AXES, split_axis=0, concat_axis=0, axis_index_groups=groups, tiled=True
    )


def cross_from_other(xl, z, y, xh, c):
    return (xl, z, y, xh, 1 - c) if c == xl else (1 - xl, z, y, xh, c)


def cross_from_same(xl, z, y, xh, c):
    return (1 - xl, z, y, xh, c) if c == xl else (xl, z, y, xh, 1 - c)


def trade_in(array):
    return permute(permute(array, cross_from_other), other_core)


def trade_out(array):
    return permute(permute(array, other_core), cross_from_same)


def other_core(xl, z, y, xh, c):
    return (xl, z, y, xh, 1 - c)


def head_groups():
    return [
        [device(xl, z, y, xh, c) for y in range(Y) for xh in range(X_HI)]
        for xl in range(X_LO)
        for z in range(Z)
        for c in range(CORE)
    ]


def column_groups():
    return [
        [device(xl, z, y, xh, c) for y in range(Y) for xh in range(X_HI) for xl in range(X_LO)]
        for z in range(Z)
        for c in range(CORE)
    ]


VMEM = pl.BlockSpec(memory_space=pltpu.VMEM)
ANY = pl.BlockSpec(memory_space=pl.ANY)


def params(mib):
    return pltpu.CompilerParams(vmem_limit_bytes=mib * 1024 * 1024)


def pack_kernel(keys, values, out, held, packed, sems):
    xl, _, _ = position()
    half = keys.shape[0] // 2
    pieces = [(kind, pl.ds(i * half, half)) for kind in range(2) for i in range(2)]
    loads, stores = [], []
    for at, (kind, rows) in enumerate(pieces):
        source = (keys, values)[kind].at[rows]
        loads.append(pltpu.make_async_copy(source, held.at[kind, rows], sems.at[0, at]))
        stores.append(
            pltpu.make_async_copy(packed.at[:, kind, rows], out.at[:, kind, rows], sems.at[1, at])
        )
        loads[at].start()
    for at, (kind, rows) in enumerate(pieces):
        loads[at].wait()
        for chip in range(Y * X_HI):
            start = pl.multiple_of((chip * 2 + xl) * HEAD_DIM, HEAD_DIM)
            packed[chip, kind, rows] = held[kind, rows, pl.ds(start, HEAD_DIM)]
        stores[at].start()
    for store in stores:
        store.wait()


def pack(keys, values):
    shape = (Y * X_HI, 2, keys.shape[0], HEAD_DIM)
    return pl.pallas_call(
        pack_kernel,
        out_shape=jax.ShapeDtypeStruct(shape, keys.dtype),
        in_specs=[ANY, ANY],
        out_specs=ANY,
        scratch_shapes=[
            pltpu.VMEM((2,) + keys.shape, keys.dtype),
            pltpu.VMEM(shape, keys.dtype),
            pltpu.SemaphoreType.DMA((2, 4)),
        ],
        compiler_params=params(56),
        name="pack",
    )(keys, values)


def select_kernel(queries, cotangents, q_came, do_came, q, do):
    xl, _, core = position()
    stay = xl == core
    q[...] = jnp.where(stay, queries[...], q_came[...])
    do[...] = jnp.where(stay, cotangents[...], do_came[...])


def select(queries, cotangents, q_came, do_came):
    out = jax.ShapeDtypeStruct(queries.shape, queries.dtype)
    return pl.pallas_call(
        select_kernel,
        out_shape=(out, out),
        in_specs=[VMEM] * 4,
        out_specs=(VMEM, VMEM),
        input_output_aliases={2: 0, 3: 1},
        compiler_params=params(8),
        cost_estimate=pl.CostEstimate(flops=0, bytes_accessed=3 * 1024 * 1024, transcendentals=0),
        name="select",
    )(queries, cotangents, q_came, do_came)


def unpack_kernel(mine, came, attended, gradients):
    xl, _, core = position()
    stay = xl == core
    attended[...] = jnp.where(stay, mine[0], came[0])
    gradients[...] = jnp.where(stay, mine[1], came[1])


def unpack(mine, came):
    out = jax.ShapeDtypeStruct(mine.shape[1:], mine.dtype)
    return pl.pallas_call(
        unpack_kernel,
        out_shape=(out, out),
        in_specs=[VMEM, VMEM],
        out_specs=(VMEM, VMEM),
        compiler_params=params(12),
        name="unpack",
    )(mine, came)


def core_sum_kernel(keep, came, up, down, across, ahead, behind, own):
    _, z, _ = position()

    def chunk(distance):
        at = lax.rem(z + distance, Z)
        return keep[at].astype(jnp.float32) + came[at].astype(jnp.float32)

    bf16 = jnp.bfloat16
    up[0] = chunk(3).astype(bf16)
    up[1] = chunk(1).astype(bf16)
    down[0] = chunk(5).astype(bf16)
    down[1] = chunk(7).astype(bf16)
    across[...] = chunk(4).astype(bf16)
    ahead[...] = chunk(2)
    behind[...] = chunk(6)
    own[...] = chunk(0)


def core_sum(keep, came):
    shape = keep.shape[1:]
    bf16, f32 = jnp.bfloat16, jnp.float32
    return pl.pallas_call(
        core_sum_kernel,
        out_shape=(
            jax.ShapeDtypeStruct((2,) + shape, bf16),
            jax.ShapeDtypeStruct((2,) + shape, bf16),
            jax.ShapeDtypeStruct(shape, bf16),
            jax.ShapeDtypeStruct(shape, f32),
            jax.ShapeDtypeStruct(shape, f32),
            jax.ShapeDtypeStruct(shape, f32),
        ),
        in_specs=[VMEM, VMEM],
        out_specs=(VMEM,) * 6,
        compiler_params=params(12),
        name="core_sum",
    )(keep, came)


def middle_sum_kernel(ahead, behind, from_below, from_above, across, up, down):
    far = across[...].astype(jnp.float32)
    first = position()[2] == 0
    zero = jnp.zeros_like(far)
    below = from_below[0].astype(jnp.float32) + jnp.where(first, far, zero)
    above = from_above[0].astype(jnp.float32) + jnp.where(first, zero, far)
    up[...] = (ahead[...] + below).astype(jnp.bfloat16)
    down[...] = (behind[...] + above).astype(jnp.bfloat16)


def middle_sum(ahead, behind, from_below, from_above, across):
    out = jax.ShapeDtypeStruct(ahead.shape, jnp.bfloat16)
    return pl.pallas_call(
        middle_sum_kernel,
        out_shape=(out, out),
        in_specs=[VMEM] * 5,
        out_specs=(VMEM, VMEM),
        compiler_params=params(12),
        name="middle_sum",
    )(ahead, behind, from_below, from_above, across)


def last_sum_kernel(own, from_below, from_above, low, high, out):
    f32 = jnp.float32
    total = own[...] + from_below[1].astype(f32) + from_above[1].astype(f32)
    total = total + low[...].astype(f32) + high[...].astype(f32)
    total = total.reshape(2, X_LO, Y * X_HI, 8, HEAD_DIM)
    for xl in range(X_LO):
        for chip in range(Y * X_HI):
            both = jnp.concatenate([total[0, xl, chip], total[1, xl, chip]], axis=0)
            out[chip * 2 + xl] = both.astype(jnp.bfloat16)


def last_sum(own, from_below, from_above, low, high):
    return pl.pallas_call(
        last_sum_kernel,
        out_shape=jax.ShapeDtypeStruct((Y * X_HI * X_LO, 16, HEAD_DIM), jnp.bfloat16),
        in_specs=[VMEM] * 5,
        out_specs=VMEM,
        compiler_params=params(12),
        name="last_sum",
    )(own, from_below, from_above, low, high)


def columns_kernel(parts, keys, values):
    for head in range(Y * X_HI * X_LO):
        both = parts[head].astype(jnp.float32)
        at = pl.ds(head * HEAD_DIM, HEAD_DIM)
        keys[:, at] = both[:8].astype(jnp.bfloat16)
        values[:, at] = both[8:].astype(jnp.bfloat16)


def columns(parts):
    out = jax.ShapeDtypeStruct((8, parts.shape[0] * HEAD_DIM), jnp.bfloat16)
    return pl.pallas_call(
        columns_kernel,
        out_shape=(out, out),
        in_specs=[VMEM],
        out_specs=(VMEM, VMEM),
        compiler_params=params(12),
        name="columns",
    )(parts)


def sum_over_z(keep, came):
    above = lambda hops: lambda xl, z, y, xh, c: (xl, (z + hops) % Z, y, xh, c)
    over = lambda xl, z, y, xh, c: (xl, (z + (2 if c == 0 else 6)) % Z, y, xh, c)
    up, down, across, ahead, behind, own = core_sum(keep, came)
    from_below = permute(up, above(1))
    from_above = permute(down, above(7))
    far = permute(across, over)
    up, down = middle_sum(ahead, behind, from_below, from_above, far)
    low = permute(up, above(2))
    high = permute(down, above(6))
    return last_sum(own, from_below, from_above, low, high)


def nt(a, b):
    return lax.dot_general(a, b, (((1,), (1,)), ((), ())), preferred_element_type=jnp.float32)


def nn(a, b):
    return jnp.dot(a, b, preferred_element_type=jnp.float32)


def half_chunks(source):
    size = CHUNK_CHIPS * source.shape[2]
    found = []
    for chip in range(0, Y * X_HI, CHUNK_CHIPS):
        load = lambda kind, chip=chip: source[chip : chip + CHUNK_CHIPS, kind].reshape(
            size, HEAD_DIM
        )
        found.append((pl.ds(len(found) * size, size), load, chip))
    return found


def scores_of(chunks, q, s_ref):
    top = None
    for rows, load, _ in chunks:
        s = nt(load(0), q)
        s_ref[rows, :] = s
        here = jnp.max(s, axis=0, keepdims=True)
        top = here if top is None else jnp.maximum(top, here)
    return top * (LOG2E * SCALE)


def weights_of(chunks, top, s_ref, e_ref):
    total, att = 0.0, 0.0
    for rows, load, _ in chunks:
        e = jnp.exp2(s_ref[rows, :] * (LOG2E * SCALE) - top)
        total = total + jnp.sum(e, axis=0, keepdims=True)
        eb = e.astype(jnp.bfloat16)
        e_ref[rows, :] = eb
        att = att + nn(load(1).T, eb)
    return total, att


def share_rows(core, full, side, first_chip, kind, keep_ref, send_ref):
    first = core == 0
    block = full.shape[0] // CHUNK_CHIPS
    full = full.reshape(CHUNK_CHIPS, block // 16, 2, 8, HEAD_DIM)
    for i in range(CHUNK_CHIPS):
        xl, low_z = divmod(first_chip + i, Y * X_HI // X_LO)
        z = low_z * 2 + side
        low = full[i, :, 0].reshape(block // 2, HEAD_DIM)
        high = full[i, :, 1].reshape(block // 2, HEAD_DIM)
        at = pl.ds(xl * (block // 2), block // 2)
        keep_ref[z, kind, at, :] = jnp.where(first, low, high).astype(jnp.bfloat16)
        send_ref[z, kind, at, :] = jnp.where(first, high, low).astype(jnp.bfloat16)


def own_half_kernel(queries, own, e_ref, att_ref, stats_ref, s_ref):
    chunks = half_chunks(own)
    top = scores_of(chunks, queries[...], s_ref)
    total, att = weights_of(chunks, top, s_ref, e_ref)
    att_ref[...] = att
    stats_ref[0:8, :] = jnp.broadcast_to(top, (8, top.shape[1]))
    stats_ref[8:16, :] = jnp.broadcast_to(total, (8, top.shape[1]))


def own_half(queries, own):
    rows = queries.shape[0]
    memory = own.shape[0] * own.shape[2]
    bf16, f32 = jnp.bfloat16, jnp.float32
    return pl.pallas_call(
        own_half_kernel,
        out_shape=(
            jax.ShapeDtypeStruct((memory, rows), bf16),
            jax.ShapeDtypeStruct((HEAD_DIM, rows), f32),
            jax.ShapeDtypeStruct((16, rows), f32),
        ),
        in_specs=[VMEM] * 2,
        out_specs=(VMEM,) * 3,
        scratch_shapes=[pltpu.VMEM((memory, rows), f32)],
        compiler_params=params(16),
        cost_estimate=pl.CostEstimate(
            flops=4 * rows * memory * HEAD_DIM,
            bytes_accessed=2 * 1024 * 1024,
            transcendentals=rows * memory,
        ),
        name="own_half",
    )(queries, own)


def both_halves_kernel(
    queries, cotangents, own, other, own_e_ref, own_att_ref, stats_ref,
    att_ref, ds_ref, keep_ref, send_ref, s_ref, e_ref,
):
    _, _, core = position()
    q = queries[...]
    chunks = half_chunks(other)
    own_top, own_total = stats_ref[0:1, :], stats_ref[8:9, :]
    top = jnp.maximum(own_top, scores_of(chunks, q, s_ref))
    total, att = weights_of(chunks, top, s_ref, e_ref)
    shrink = jnp.exp2(own_top - top)
    inverse = 1.0 / (own_total * shrink + total)
    att = (own_att_ref[...] * shrink + att) * inverse
    att_ref[...] = att.T.astype(jnp.bfloat16)
    dot = cotangents[...].astype(jnp.float32).T * inverse
    half = own_e_ref.shape[0]
    for base, source, side, weights, scaled in (
        (0, own, core, own_e_ref, dot * shrink),
        (half, other, 1 - core, e_ref, dot),
    ):
        scaled = scaled.astype(jnp.bfloat16)
        delta = jnp.sum(att * scaled.astype(jnp.float32), axis=0, keepdims=True)
        rows_scaled = scaled.T
        for rows, load, chip in half_chunks(source):
            e = weights[rows, :]
            dp = nn(load(1), scaled)
            ds = (e.astype(jnp.float32) * (dp - delta)).astype(jnp.bfloat16)
            ds_ref[pl.ds(base + rows.start, rows.size), :] = ds
            share_rows(core, nn(ds, q) * SCALE, side, chip, 0, keep_ref, send_ref)
            share_rows(core, nn(e, rows_scaled), side, chip, 1, keep_ref, send_ref)


def both_halves(queries, cotangents, own, other, own_e, own_att, stats):
    half, rows = own_e.shape
    bf16, f32 = jnp.bfloat16, jnp.float32
    parts = jax.ShapeDtypeStruct((Z, 2, 2 * half // (2 * Z), HEAD_DIM), bf16)
    return pl.pallas_call(
        both_halves_kernel,
        out_shape=(
            jax.ShapeDtypeStruct((rows, HEAD_DIM), bf16),
            jax.ShapeDtypeStruct((2 * half, rows), bf16),
            parts,
            parts,
        ),
        in_specs=[VMEM] * 7,
        out_specs=(VMEM,) * 4,
        scratch_shapes=[pltpu.VMEM((half, rows), f32), pltpu.VMEM((half, rows), bf16)],
        compiler_params=params(20),
        cost_estimate=pl.CostEstimate(
            flops=12 * rows * half * HEAD_DIM,
            bytes_accessed=4 * 1024 * 1024,
            transcendentals=rows * half,
        ),
        name="both_halves",
    )(queries, cotangents, own, other, own_e, own_att, stats)


def queries_kernel(own, other, ds_ref, att_ref, rows_out):
    rows_out[0] = att_ref[...]
    dq = 0.0
    base = 0
    for source in (own, other):
        for rows, load, _ in half_chunks(source):
            dq = dq + nn(load(0).T, ds_ref[pl.ds(base + rows.start, rows.size), :])
        base = ds_ref.shape[0] // 2
    rows_out[1] = (dq * SCALE).T.astype(jnp.bfloat16)


def queries_step(own, other, ds, att):
    memory, rows = ds.shape
    return pl.pallas_call(
        queries_kernel,
        out_shape=jax.ShapeDtypeStruct((2,) + att.shape, att.dtype),
        in_specs=[VMEM] * 4,
        out_specs=VMEM,
        compiler_params=params(12),
        cost_estimate=pl.CostEstimate(
            flops=2 * rows * memory * HEAD_DIM, bytes_accessed=2 * 1024 * 1024, transcendentals=0
        ),
        name="queries_step",
    )(own, other, ds, att)


def per_device(queries, mem_keys, mem_values, grad_out):
    q, do = select(queries, grad_out, trade_in(queries), trade_in(grad_out))
    own = exchange(pack(mem_keys, mem_values), head_groups())
    own, q, do = lax.optimization_barrier((own, q, do))
    other = permute(own, other_core)
    att, ds, keep, send = both_halves(q, do, own, other, *own_half(q, own))
    came = permute(send, other_core)
    rows = queries_step(own, other, ds, att)
    traded = trade_out(rows)
    sums = sum_over_z(keep, came)
    attended, query_gradients = unpack(rows, traded)
    grad_keys, grad_values = columns(exchange(sums, column_groups()))
    return attended, query_gradients, grad_keys, grad_values


def solution(mesh):
    in_specs = (P("query", "head"), P("head", None), P("head", None), P("query", "head"))
    out_specs = (
        P("query", "head"),
        P("query", "head"),
        P(("query", "head"), None),
        P(("query", "head"), None),
    )
    return jax.shard_map(
        per_device, mesh=mesh, in_specs=in_specs, out_specs=out_specs, check_vma=False
    )
```
